32 devices in a mesh: groups: 2 (over x), clus: 16 (over z, y, core).
Axes of the slice: x: 2, y: 2, z: 4, core: 2. Of those that a mesh axis runs over, the one named last changes fastest.
Arguments:
- adjoint_volume: float32 [256, 128, 128], P(('groups', 'clus')), parts along dimension 0, may hold values from -6 to 6
- stiffness: float32 [256, 128, 128], P(('groups', 'clus')), parts along dimension 0, may hold values from 0.2 to 4
- boundary_source: bfloat16 [512, 256, 128], P(('groups', 'clus')), parts along dimension 0, may hold values from -6 to 6
- trace_gain: float32 [128], replicated, may hold values from 0.03 to 0.3
- trace_map: int32 [512, 256], P(('groups', 'clus')), parts along dimension 0, may hold values from 0 to 16383
- near_blocks: bfloat16 [2048, 256, 256], P(('groups', 'clus')), parts along dimension 0, may hold values from -0.375 to 0.375
- near_source: int32 [2048], P(('groups', 'clus')), parts along dimension 0, may hold values from 0 to 15
- near_target_dev: int32 [2048, 1], P(('groups', 'clus')), parts along dimension 0, may hold values from 0 to 15; in each aligned block of 64 rows (0 to 63, 64 to 127, ...) at most 8 rows name the same one
- near_target_local: int32 [2048], P(('groups', 'clus')), parts along dimension 0, may hold values from 0 to 15
- close_block_column_count: int32 [2048], P(('groups', 'clus')), parts along dimension 0, may hold values from 64 to 256
- far_basis_in: bfloat16 [2048, 16, 256], P(('groups', 'clus')), parts along dimension 0, may hold values from -0.375 to 0.375
- far_basis_out: bfloat16 [2048, 16, 256], P(('groups', 'clus')), parts along dimension 0, may hold values from -1.5 to 1.5
- far_source: int32 [2048], P(('groups', 'clus')), parts along dimension 0, may hold values from 0 to 15
- far_target_dev: int32 [2048, 1], P(('groups', 'clus')), parts along dimension 0, may hold values from 0 to 15; in each aligned block of 64 rows (0 to 63, 64 to 127, ...) at most 10 rows name the same one
- far_target_local: int32 [2048], P(('groups', 'clus')), parts along dimension 0, may hold values from 0 to 15
Outputs:
- stencil_volume_image: float32 [256, 128, 128], P(('groups', 'clus')), parts along dimension 0
- boundary_image: float32 [512, 256, 128], P(('groups', 'clus')), parts along dimension 0
The draws below stay inside these ranges and needn't reach their ends.
There are 2 independent parts, one for each index of `groups`. The reference program is written for one: setup_inputs(seed, part) draws one part's arguments, and reference() takes and returns one part's arrays. A program takes and returns all parts, laid end to end along the dimension named above; an argument that names none is the same for every part. Nothing has to cross between parts.
Inputs may be any that keep to these rules, and one draw needn't show every extreme that they name: `near_target_dev`: in the rows of one device no owner is named by more than 8 rows, and some owner is named by exactly that many. `far_target_dev`: in the rows of one device no owner is named by more than 10 rows.
All inputs are finite; a program needn't handle non-finite values.
Results may differ from the reference program's by a relative error of at most 0.0044.
Values may be sent and summed in bfloat16 or wider, within the bound.
No kernel may reach another device: no remote copies, remote signals or barrier semaphores. Data moves between devices by JAX's collectives and lax.ppermute only.
A program may use at most 128 MiB of HBM per device.

```python
import math
import jax
import jax.numpy as jnp
import numpy as np
from jax import lax

B = 256
K = 16
R = 128
CLU_DEV = 16
NEAR_DEV = 64
FAR_DEV = 64
CY = 128
CZ = 128
NX = 128
CLUSTERS = 256
NEARS = 1024
FARS = 1024
NEAR_CAP = 8
FAR_CAP = 10
N_CLUS = 16


def plant(entries, stream_key, smallest, top_value):
    spot = [jax.random.randint(jax.random.fold_in(stream_key, axis), (), 0, length) for axis, length in enumerate(entries.shape)]
    main_axis = entries.shape.index(max(entries.shape))
    neighbour = spot[:main_axis] + [(spot[main_axis] + 1) % entries.shape[main_axis]] + spot[main_axis + 1:]
    return entries.at[tuple(spot)].set(smallest).at[tuple(neighbour)].set(top_value)


def levels(own_key, dims, cuts, smallest, top_value):
    factor_of = 1.0
    for axis_at, parts in cuts:
        steps = jax.random.uniform(jax.random.fold_in(jax.random.fold_in(own_key, 6), axis_at), (parts,), jnp.float32, smallest / len(cuts), top_value / len(cuts))
        factor_of = factor_of * jnp.repeat(jnp.exp(steps), dims[axis_at] // parts).reshape((-1,) + (1,) * (len(dims) - 1 - axis_at))
    return factor_of


def assign_block(own_key, own, number, rows, number_of, top, reach, skew):
    sequence = jax.random.permutation(own_key, number_of)
    heavy_load, ordinary = shares(number_of, rows * top, reach, skew, True), shares(number_of, rows * top, reach, skew, False)
    places = jnp.arange(number_of)

    def named(lengths, offset_by):
        used = int((lengths > 0).sum())
        fixed = max(1, used // 4)
        moved = fixed + (places - fixed + offset_by * (used - fixed)) % max(1, number_of - fixed)
        return jnp.zeros((number_of,), jnp.int32).at[sequence[jnp.where(places < fixed, places, moved)]].set(jnp.asarray(lengths, jnp.int32))

    lengths = jnp.where(number % 4 == 0, named(heavy_load, number // 4), named(ordinary, number - number // 4 - 1))
    mixed = jax.random.permutation(jax.random.fold_in(own, 3), number_of)
    donor, receiver = mixed[0:number_of // 2 * 2:2], mixed[1:number_of // 2 * 2:2]
    room = jnp.minimum(lengths[donor] - 1, reach - lengths[receiver]) // 2
    room = jnp.where((donor == sequence[0]) | (receiver == sequence[0]) | (lengths[receiver] == 0), 0, jnp.maximum(room, 0))
    moved = jax.random.randint(jax.random.fold_in(own, 4), (number_of // 2,), 0, 1 << 20) % (room + 1)
    lengths = lengths.at[donor].add(-moved).at[receiver].add(moved)
    members = jnp.searchsorted(jnp.cumsum(lengths), jnp.arange(rows * top), side="right").astype(jnp.int32)
    listing = members.reshape(top, rows).T
    listing = listing[jax.random.permutation(jax.random.fold_in(own, 1), rows)]
    offset_by = jax.random.randint(jax.random.fold_in(own, 2), (rows, 1), 0, top)
    return jnp.take_along_axis(listing, (jnp.arange(top)[None, :] + offset_by) % top, axis=1)


def shares(count, total, reach, slope, full):
    loads = [(1 << 20) // math.isqrt(standing ** slope) + 1 for standing in range(1, count + 1)]
    largest = reach if full else min(reach, max(-(-total // count), total * loads[0] // sum(loads)))
    least = 1 if total - largest >= count - 1 else 0
    counts, rest = [largest] + [least] * (count - 1), total - largest - least * (count - 1)
    while rest > 0:
        candidates = [i for i in range(1, count) if counts[i] < largest] or [i for i in range(1, count) if counts[i] < reach]
        mass, budget = sum([loads[i] for i in candidates]), rest
        for i in candidates:
            addition = min(reach - counts[i], max(1, budget * loads[i] // mass), rest)
            counts[i] = counts[i] + addition
            rest = rest - addition
    return np.array(counts)


def gaussian(own_key, shape, deviation, most, shards=(), held_as=jnp.bfloat16):
    factor_of = levels(own_key, shape, shards, -0.22, 0.18) if shards else 1.0
    drawn = jax.random.normal(own_key, shape, jnp.float32) * deviation * factor_of
    return jnp.minimum(jnp.maximum(drawn, -most), most).astype(held_as)


def setup_inputs(seed: int = 0, part: int = 0) -> dict:
    key_of = jax.random.split(jax.random.key(seed), 16)
    part_splits = jax.random.split(jax.random.fold_in(key_of[15], part), 16)
    adjoint_volume = gaussian(part_splits[0], (NX, CY, CZ), 1.0, 6.0, ((0, 16),), jnp.float32)
    stiffness = jnp.clip(jnp.exp(math.log(4.0) - 2.9957323 * jax.random.uniform(part_splits[1], (NX, CY, CZ), jnp.float32) ** levels(part_splits[1], (NX, CY, CZ), ((0, 16),), -0.2, 0.2)), 0.2, 4.0)
    boundary_source = gaussian(part_splits[2], (CLUSTERS, B, R), 1.0, 6.0, ((0, 16),))
    trace_gain = jnp.clip(jnp.exp(jax.random.uniform(key_of[3], (R,), jnp.float32, math.log(0.03), math.log(0.3))), 0.03, 0.3)
    trace_map = plant(jax.random.randint(part_splits[4], (CLUSTERS, B), 0, NX * CY), jax.random.fold_in(part_splits[4], 1), 0, (NX * CY) - 1).astype(jnp.int32)
    near_blocks = gaussian(part_splits[5], (NEARS, B, B), B ** -0.5, 0.375, ((0, 16),))
    near_source = plant(jax.random.randint(part_splits[6], (NEARS,), 0, CLU_DEV), jax.random.fold_in(part_splits[6], 1), 0, CLU_DEV - 1).astype(jnp.int32)
    near_target_dev_keys = jax.random.split(jax.random.fold_in(part_splits[7], 1), NEARS // NEAR_DEV)
    near_target_dev_turns = jax.random.permutation(jax.random.fold_in(part_splits[7], 3), NEARS // NEAR_DEV)
    near_target_dev = jax.vmap(lambda own, number: assign_block(jax.random.fold_in(part_splits[7], 2), own, number, NEAR_DEV, N_CLUS, 1, NEAR_CAP, 2))(near_target_dev_keys, near_target_dev_turns).reshape((NEARS, 1))
    near_target_local = plant(jax.random.randint(part_splits[8], (NEARS,), 0, CLU_DEV), jax.random.fold_in(part_splits[8], 1), 0, CLU_DEV - 1).astype(jnp.int32)
    close_block_column_count = plant(jax.random.randint(part_splits[9], (NEARS,), B // 4, B + 1), jax.random.fold_in(part_splits[9], 1), B // 4, B).astype(jnp.int32)
    far_basis_in = gaussian(part_splits[10], (FARS, K, B), B ** -0.5, 0.375, ((0, 16),))
    far_basis_out = gaussian(part_splits[11], (FARS, K, B), K ** -0.5, 1.5, ((0, 16),))
    far_source = plant(jax.random.randint(part_splits[12], (FARS,), 0, CLU_DEV), jax.random.fold_in(part_splits[12], 1), 0, CLU_DEV - 1).astype(jnp.int32)
    far_target_dev_keys = jax.random.split(jax.random.fold_in(part_splits[13], 1), FARS // FAR_DEV)
    far_target_dev_turns = jax.random.permutation(jax.random.fold_in(part_splits[13], 3), FARS // FAR_DEV)
    far_target_dev = jax.vmap(lambda own, number: assign_block(jax.random.fold_in(part_splits[13], 2), own, number, FAR_DEV, N_CLUS, 1, FAR_CAP, 1))(far_target_dev_keys, far_target_dev_turns).reshape((FARS, 1))
    far_target_local = plant(jax.random.randint(part_splits[14], (FARS,), 0, CLU_DEV), jax.random.fold_in(part_splits[14], 1), 0, CLU_DEV - 1).astype(jnp.int32)
    return dict(adjoint_volume=adjoint_volume, stiffness=stiffness, boundary_source=boundary_source, trace_gain=trace_gain, trace_map=trace_map, near_blocks=near_blocks, near_source=near_source, near_target_dev=near_target_dev, near_target_local=near_target_local, close_block_column_count=close_block_column_count, far_basis_in=far_basis_in, far_basis_out=far_basis_out, far_source=far_source, far_target_dev=far_target_dev, far_target_local=far_target_local)


def stencil_matrix(field, coefficient):
    padded = jnp.pad(field, 1)
    beside = padded[2:, 1:-1, 1:-1] + padded[:-2, 1:-1, 1:-1]
    beside = beside + padded[1:-1, 2:, 1:-1] + padded[1:-1, :-2, 1:-1]
    beside = beside + padded[1:-1, 1:-1, 2:] + padded[1:-1, 1:-1, :-2]
    return (6.0 + coefficient) * field - beside


def reference(adjoint_volume, stiffness, boundary_source, trace_gain, trace_map, near_blocks, near_source, near_target_dev, near_target_local, close_block_column_count, far_basis_in, far_basis_out, far_source, far_target_dev, far_target_local):
    stencil_volume_image = stencil_matrix(adjoint_volume, stiffness)
    face = stencil_volume_image[:, :, 0].reshape(-1)
    traces = face[trace_map]
    driven_values = boundary_source.astype(jnp.float32) + traces[:, :, None] * trace_gain[None, None, :]
    unknowns = driven_values.astype(jnp.bfloat16)
    total_clusters = CLU_DEV * N_CLUS
    by_device = unknowns.reshape(N_CLUS, CLU_DEV, B, R)
    columns = jnp.arange(B, dtype=jnp.int32)

    def near_step(total, inputs):
        blocks, source, owner, local, count, local_unknowns = inputs
        chosen = local_unknowns[source]
        chosen = jnp.where((columns[None, :] < count[:, None])[:, :, None], chosen, jnp.zeros_like(chosen))
        product = jnp.einsum("pij,pjr->pir", blocks.astype(jnp.float32), chosen.astype(jnp.float32))
        rounded = lax.optimization_barrier(product.astype(jnp.bfloat16))
        target = (owner[:, 0] * CLU_DEV + local).astype(jnp.int32)
        return total + jax.ops.segment_sum(rounded.astype(jnp.float32), target, num_segments=total_clusters), None

    def far_step(total, inputs):
        basis_in, basis_out, source, owner, local, local_unknowns = inputs
        chosen = local_unknowns[source]
        coeff = jnp.einsum("pkb,pbr->pkr", basis_in.astype(jnp.float32), chosen.astype(jnp.float32))
        coeff = lax.optimization_barrier(coeff.astype(jnp.bfloat16))
        expanded = jnp.einsum("pkb,pkr->pbr", basis_out.astype(jnp.float32), coeff.astype(jnp.float32))
        rounded = lax.optimization_barrier(expanded.astype(jnp.bfloat16))
        target = (owner[:, 0] * CLU_DEV + local).astype(jnp.int32)
        return total + jax.ops.segment_sum(rounded.astype(jnp.float32), target, num_segments=total_clusters), None

    start = jnp.zeros((total_clusters, B, R), jnp.float32)
    close_block_total, _ = lax.scan(near_step, start, (
        near_blocks.reshape(N_CLUS, NEAR_DEV, B, B), near_source.reshape(N_CLUS, NEAR_DEV),
        near_target_dev.reshape(N_CLUS, NEAR_DEV, 1), near_target_local.reshape(N_CLUS, NEAR_DEV),
        close_block_column_count.reshape(N_CLUS, NEAR_DEV), by_device))
    far_total, _ = lax.scan(far_step, start, (
        far_basis_in.reshape(N_CLUS, FAR_DEV, K, B), far_basis_out.reshape(N_CLUS, FAR_DEV, K, B),
        far_source.reshape(N_CLUS, FAR_DEV), far_target_dev.reshape(N_CLUS, FAR_DEV, 1),
        far_target_local.reshape(N_CLUS, FAR_DEV), by_device))
    return stencil_volume_image, driven_values + close_block_total + far_total
```

```python
import functools

import jax
import jax.numpy as jnp
from jax import lax
from jax.experimental import pallas as pl
from jax.experimental.pallas import tpu as pltpu
from jax.sharding import PartitionSpec as P

F32 = jnp.float32
BF16 = jnp.bfloat16
I32 = jnp.int32
MIB = 1 << 20

PLAN = ((2, "yz"), (2, "zy"), (4, "yz"), (4, "yz"), (4, "yz"))


def smem():
    return pl.BlockSpec(memory_space=pltpu.SMEM)


def vmem():
    return pl.BlockSpec(memory_space=pltpu.VMEM)


def iota(shape, dim):
    return lax.broadcasted_iota(I32, shape, dim)


def pieces(value, count):
    out = []
    for _ in range(count):
        part = value.astype(BF16)
        out.append(part)
        value = value - part.astype(F32)
    return out


def chunk_kernel(
    first, size, peers, ns, nd, nl, count, fs, fd, fl, source, basis_in, basis_out, blocks,
    send, keep, total, held, near_list, far_list, sems,
):
    me = lax.axis_index("clus")
    lines = peers // 4
    half = peers // 2 * size

    def compact(local, listing, pairs):
        def step(p, found):
            mine = local[p]
            listing[found] = p
            return found + jnp.where((mine >= first) & (mine < first + size), 1, 0)

        return lax.fori_loop(0, pairs, step, 0)

    nears = compact(nl, near_list, nl.shape[0])

    def fetch(i):
        return pltpu.make_async_copy(blocks.at[near_list[i]], held.at[i], sems.at[i])

    @pl.loop(0, nears)
    def _(i):
        fetch(i).start()

    fars = compact(fl, far_list, fl.shape[0])

    @pl.loop(0, total.shape[0])
    def _(i):
        total[i] = jnp.zeros(total.shape[1:], F32)

    def slot(device, local):
        apart = device ^ me
        place = ((apart >> 1) & 1) * lines + (apart >> 2)
        return (apart & 1) * half + place * size + local - first

    @pl.loop(0, fars)
    def _(i):
        p = far_list[i]
        coefficients = jnp.dot(basis_in[p], source[fs[p]], preferred_element_type=F32)
        stacked = jnp.concatenate(pieces(coefficients, 2), axis=0)
        basis = jnp.concatenate([basis_out[p], basis_out[p]], axis=0)
        part = lax.dot_general(basis, stacked, (((0,), (0,)), ((), ())), preferred_element_type=F32)
        at = slot(fd[p], fl[p])
        total[at] = total[at] + part

    rows = iota(source.shape[1:], 0)

    @pl.loop(0, nears)
    def _(i):
        p = near_list[i]
        chosen = jnp.where(rows < count[p], source[ns[p]].astype(F32), 0.0).astype(BF16)
        at = slot(nd[p], nl[p])
        fetch(i).wait()
        total[at] = total[at] + jnp.dot(held[i], chosen, preferred_element_type=F32)

    @pl.loop(0, half)
    def _(i):
        keep[i] = total[i].astype(BF16)
        send[i] = total[half + i].astype(BF16)


def chunk_sums(first, size, peers, scalars, source, basis_in, basis_out, blocks):
    pairs, width, _ = blocks.shape
    far_pairs = basis_in.shape[0]
    depth = source.shape[2]
    tiles = jax.ShapeDtypeStruct((peers // 2 * size, width, depth), BF16)
    send, keep = pl.pallas_call(
        functools.partial(chunk_kernel, first, size, peers),
        out_shape=(tiles, tiles),
        in_specs=[smem()] * 7 + [vmem()] * 3 + [pl.BlockSpec(memory_space=pl.ANY)],
        out_specs=(vmem(), vmem()),
        scratch_shapes=[
            pltpu.VMEM((peers * size, width, depth), F32),
            pltpu.VMEM((pairs, width, width), BF16),
            pltpu.SMEM((pairs + 1,), I32),
            pltpu.SMEM((far_pairs + 1,), I32),
            pltpu.SemaphoreType.DMA((pairs,)),
        ],
        compiler_params=pltpu.CompilerParams(vmem_limit_bytes=48 * MIB),
        cost_estimate=pl.CostEstimate(flops=2 * 10**9 // 8, bytes_accessed=12 * MIB, transcendentals=0),
        name="dense_sums",
    )(*scalars, source, basis_in, basis_out, blocks)
    shape = (2, peers // 4, size, width, depth)
    return send.reshape(shape), keep.reshape(shape)


def pack_kernel(volume, stiffness, out):
    planes, cy, cz = volume.shape
    lanes = iota((cy, cz), 1)
    packed = jnp.zeros((cy, cz), F32)
    rows = iota((cy, cz), 0)

    def place(packed, column, at):
        return jnp.where(lanes == at, column, packed)

    for x in range(planes):
        here = volume[x]
        beside = jnp.where(rows == 0, 0.0, pltpu.roll(here, 1, 0))
        beside = beside + jnp.where(rows == cy - 1, 0.0, pltpu.roll(here, cy - 1, 0))
        if x > 0:
            beside = beside + volume[x - 1]
        if x < planes - 1:
            beside = beside + volume[x + 1]
        face = (6.0 + stiffness[x]) * here - beside
        column = face[:, 0:1] - here[:, 1:2]
        packed = place(packed, column, x)
    packed = place(packed, volume[0][:, 0:1], planes)
    packed = place(packed, volume[planes - 1][:, 0:1], planes + 1)
    out[...] = packed.T[: out.shape[0]]


def pack_face(volume, stiffness):
    planes, cy, cz = volume.shape
    return pl.pallas_call(
        pack_kernel,
        out_shape=jax.ShapeDtypeStruct((-(-(planes + 2) // 8) * 8, cy), F32),
        in_specs=[vmem()] * 2,
        out_specs=vmem(),
        name="pack_face",
    )(volume, stiffness)


def stencil_kernel(volume, stiffness, before, after, out):
    planes, cy, cz = volume.shape
    rows = iota((cy, cz), 0)
    lanes = iota((cy, cz), 1)
    for x in range(planes):
        here = volume[x]
        beside = (volume[x + 1] if x < planes - 1 else after[0]) + (volume[x - 1] if x > 0 else before[0])
        beside = beside + jnp.where(rows == cy - 1, 0.0, pltpu.roll(here, cy - 1, 0))
        beside = beside + jnp.where(rows == 0, 0.0, pltpu.roll(here, 1, 0))
        beside = beside + jnp.where(lanes == cz - 1, 0.0, pltpu.roll(here, cz - 1, 1))
        beside = beside + jnp.where(lanes == 0, 0.0, pltpu.roll(here, 1, 1))
        out[x] = (6.0 + stiffness[x]) * here - beside


def stencil(volume, stiffness, before, after):
    return pl.pallas_call(
        stencil_kernel,
        out_shape=jax.ShapeDtypeStruct(volume.shape, F32),
        in_specs=[vmem()] * 4,
        out_specs=vmem(),
        name="stencil",
    )(volume, stiffness, before, after)


def trace_kernel(
    ns, target, count, packs, places, near_blocks, basis_in, basis_out, far_source, far_target,
    traces, images, face,
):
    peers, _, cy = packs.shape
    nx = face.shape[0]
    planes = nx // peers
    clusters, width = places.shape
    rows8 = iota((planes, cy), 0)
    for n in range(peers):
        part = packs[n, 0:planes, :]
        if n > 0:
            part = part - jnp.where(rows8 == 0, packs[n - 1, planes + 1 : planes + 2, :], 0.0)
        if n < peers - 1:
            part = part - jnp.where(rows8 == planes - 1, packs[n + 1, planes : planes + 1, :], 0.0)
        face[n * planes : (n + 1) * planes, :] = part
    turned = jnp.concatenate(pieces(face[...].T, 3), axis=0)
    x_rows = iota((nx, width), 0)
    y_rows = iota((cy, width), 0)
    shift = cy.bit_length() - 1

    @pl.loop(0, clusters)
    def _(c):
        place = places[pl.ds(c, 1), :]
        picks = jnp.where(x_rows == (place >> shift), 1.0, 0.0).astype(BF16)
        columns = jnp.dot(turned, picks, preferred_element_type=F32)
        columns = columns[:cy] + columns[cy : 2 * cy] + columns[2 * cy :]
        found = jnp.where(y_rows == (place & (cy - 1)), columns, 0.0)
        traces[pl.ds(c, 1), :] = jnp.sum(found, axis=0, keepdims=True)

    contract = (((1,), (1,)), ((), ()))
    stacked = jnp.concatenate(pieces(traces[...], 2), axis=0)
    coefficients = lax.dot_general(stacked, basis_in[...], contract, preferred_element_type=F32)
    coefficients = coefficients[:clusters] + coefficients[clusters:]
    pairs_k = coefficients.shape[1]
    coefficients = jnp.where(iota((clusters, pairs_k), 0) == far_source[...], coefficients, 0.0)
    coefficients = jnp.sum(coefficients, axis=0, keepdims=True)
    block = 128

    @pl.loop(0, images.shape[0] // block)
    def _(b):
        base = pl.multiple_of(b * block, block)
        spread = jnp.where(iota((block, pairs_k), 0) + base == far_target[...], coefficients, 0.0)
        image = jnp.zeros((block, width), F32)
        for part in pieces(spread, 2):
            image = image + jnp.dot(part, basis_out[...], preferred_element_type=F32)
        images[pl.ds(base, block), :] = image

    lanes = iota((8, width), 1)
    rows = iota((8, width), 0)

    @pl.loop(0, near_blocks.shape[0])
    def _(p):
        at = target[p]
        base = pl.multiple_of((at >> 3) * 8, 8)
        trace = traces[pl.ds(ns[p], 1), :]
        placed = jnp.where((rows == (at & 7)) & (lanes < count[p]), trace, 0.0)
        both = jnp.concatenate(pieces(placed, 2), axis=0)
        image = lax.dot_general(both, near_blocks[p], contract, preferred_element_type=F32)
        images[pl.ds(base, 8), :] = images[pl.ds(base, 8), :] + (image[:8] + image[8:])


def trace_images(peers, nx, ns, target, count, packs, places, near_blocks, basis_in, basis_out, far_source, far_target):
    clusters, width = places.shape
    pairs, rank, _ = basis_in.shape
    return pl.pallas_call(
        trace_kernel,
        out_shape=(
            jax.ShapeDtypeStruct((clusters, width), F32),
            jax.ShapeDtypeStruct((peers * clusters, width), F32),
        ),
        in_specs=[smem()] * 3 + [vmem()] * 7,
        out_specs=(vmem(), vmem()),
        scratch_shapes=[pltpu.VMEM((nx, packs.shape[2]), F32)],
        compiler_params=pltpu.CompilerParams(vmem_limit_bytes=32 * MIB),
        cost_estimate=pl.CostEstimate(flops=2 * 10**9, bytes_accessed=12 * MIB, transcendentals=0),
        name="trace_images",
    )(
        ns, target, count, packs, places, near_blocks,
        basis_in.reshape(pairs * rank, width), basis_out.reshape(pairs * rank, width),
        jnp.repeat(far_source, rank)[None, :], jnp.repeat(far_target, rank)[None, :],
    )


def add(*terms):
    out = terms[0].astype(F32)
    for term in terms[1:]:
        out = out + term.astype(F32)
    return out


def swap(value, bit):
    peers = lax.axis_size("clus")
    return lax.ppermute(value, "clus", [(i, i ^ bit) for i in range(peers)])


def z_terms(parts):
    peers = lax.axis_size("clus")
    lines = peers // 4
    if lines != 4:
        terms = [parts(0)]
        for k in range(1, lines):
            terms.append(swap(parts(k).astype(BF16), 4 * k))
        return terms
    up = [(i, i + 4) for i in range(peers)]
    down = [(i, i - 4) for i in range(peers)]
    outer = jnp.stack([parts(1), parts(2), parts(3)]).astype(BF16)
    outer = lax.ppermute(outer, "clus", up[0:4] + down[12:16])
    middle = jnp.stack([add(parts(3), outer[1]), add(parts(2), outer[2])]).astype(BF16)
    middle = lax.ppermute(middle, "clus", up[4:8] + down[8:12])
    inner = add(parts(1), middle[1]).astype(BF16)
    inner = lax.ppermute(inner, "clus", down[4:8] + up[8:12])
    return [parts(0), outer[0], middle[0], inner]


def body(
    adjoint_volume,
    stiffness,
    boundary_source,
    trace_gain,
    trace_map,
    near_blocks,
    near_source,
    near_target_dev,
    near_target_local,
    close_block_column_count,
    far_basis_in,
    far_basis_out,
    far_source,
    far_target_dev,
    far_target_local,
):
    peers = lax.axis_size("clus")
    clusters = boundary_source.shape[0]
    planes = adjoint_volume.shape[0]
    near_owner = near_target_dev.reshape(-1)
    far_owner = far_target_dev.reshape(-1)
    scalars = (
        near_source, near_owner, near_target_local, close_block_column_count,
        far_source, far_owner, far_target_local,
    )

    spans = []
    first = 0
    for share, order in PLAN:
        size = share * clusters // 16
        spans.append((first, size, order))
        first += size

    sums = []
    for first, size, order in spans:
        send, keep = chunk_sums(first, size, peers, scalars, boundary_source, far_basis_in, far_basis_out, near_blocks)
        sums.append((keep, swap(send, 1)))

    ends = peers - 1
    before = lax.ppermute(adjoint_volume[planes - 1 :], "clus", [(i, i + 1) for i in range(ends)])
    after = lax.ppermute(adjoint_volume[:1], "clus", [(i + 1, i) for i in range(ends)])
    packed = pack_face(adjoint_volume, stiffness)
    packs = lax.all_to_all(
        jnp.broadcast_to(packed[None], (peers,) + packed.shape), "clus", split_axis=0, concat_axis=0, tiled=True
    )
    stencil_volume_image = stencil(adjoint_volume, stiffness, before, after)
    traces, images = trace_images(
        peers, planes * peers, near_source, near_owner * clusters + near_target_local, close_block_column_count,
        packs, trace_map, near_blocks, far_basis_in, far_basis_out, far_source, far_owner * clusters + far_target_local,
    )
    images = lax.all_to_all(
        images.reshape((peers, clusters) + images.shape[1:]), "clus", split_axis=0, concat_axis=0, tiled=True
    )
    vectors = traces + jnp.sum(images, axis=0)

    outs = []
    for (first, size, order), (keep, got) in zip(spans, sums):
        if order == "yz":
            across = swap(add(keep[1], got[1]).astype(BF16), 2)
            terms = z_terms(lambda k: add(keep[0, k], got[0, k], across[k]))
        else:
            other = z_terms(lambda k: add(keep[:, k], got[:, k]))
            total = add(*other)
            terms = [total[0], swap(total[1].astype(BF16), 2)]
        here = slice(first, first + size)
        outs.append(add(boundary_source[here], *terms) + vectors[here][:, :, None] * trace_gain[None, None, :])
    return (stencil_volume_image, jnp.concatenate(outs, axis=0))


def solution(mesh):
    whole = ("groups", "clus")
    one, two, three = P(whole), P(whole, None), P(whole, None, None)
    return jax.shard_map(
        body,
        mesh=mesh,
        in_specs=(three, three, three, P(), two, three, one, two, one, one, three, three, one, two, one),
        out_specs=(three, three),
        check_vma=False,
    )
```

```python
import functools

import jax
import jax.numpy as jnp
from jax import lax
from jax.experimental import pallas as pl
from jax.experimental.pallas import tpu as pltpu
from jax.sharding import PartitionSpec as P

F32 = jnp.float32
BF16 = jnp.bfloat16
I32 = jnp.int32
MIB = 1 << 20
VMEM_BYTES = 60 * MIB
NO_COST = pl.CostEstimate(flops=1, bytes_accessed=1, transcendentals=0)

PLAN = ((6, False, 0), (5, False, 1), (3, False, 1), (2, False, 1))

SEQUENCE = tuple("s00s123fw10fbw210fvw3210vw321w32w3")


def smem():
    return pl.BlockSpec(memory_space=pltpu.SMEM)


def vmem():
    return pl.BlockSpec(memory_space=pltpu.VMEM)


def iota(shape, dim):
    return lax.broadcasted_iota(I32, shape, dim)


def pieces(value, count):
    out = []
    for _ in range(count):
        part = value.astype(BF16)
        out.append(part)
        value = value - part.astype(F32)
    return out


GROUP = 4


def order_of(peers, z_first):
    z = []
    bit = 4
    while bit < peers:
        z.append(bit)
        bit *= 2
    return [1] + z + [2] if z_first else [1, 2] + z


def place_of(apart, bits):
    place = 0
    for bit in bits:
        place = place * 2 + jnp.where((apart & bit) != 0, 1, 0)
    return place


def ranges(peers):
    return ((peers // 2, 3 * peers // 4), (3 * peers // 4, peers), (0, peers // 2))


def sums_kernel(spans, peers, near_pairs, far_pairs, table, far_source, far_in, far_out, blocks, *refs):
    parts = ranges(peers)
    outs = refs[: len(spans) * len(parts)]
    (total, held, coefficients, zeros, staged, source, basis_in, basis_out, near_list, far_list, rank, tile,
     load_sems, block_sems, zero_sems, tile_sems) = refs[len(outs) :]
    loads = [
        pltpu.make_async_copy(whole, part, load_sems.at[i])
        for i, (whole, part) in enumerate(((far_source, source), (far_in, basis_in), (far_out, basis_out)))
    ]
    for load in loads:
        load.start()
    me = lax.axis_index("clus")
    half = peers // 2
    first = spans[0][0]
    size = sum(length for _, length, _ in spans)
    tiles = peers * size
    ns, nd, nl, count, fs, fd, fl = [
        (lambda at: lambda p: table[at + p])(at)
        for at in (0, near_pairs, 2 * near_pairs, 3 * near_pairs, 4 * near_pairs, 4 * near_pairs + far_pairs, 4 * near_pairs + 2 * far_pairs)
    ]
    spare = total.shape[0] - 1

    def compact(local, listing, pairs):
        def step(p, found):
            at = local(p)
            listing[found] = p
            return found + jnp.where((at >= first) & (at < first + size), 1, 0)

        found = lax.fori_loop(0, pairs, step, 0, unroll=8)
        for u in range(GROUP):
            listing[found + u] = 0
        return found

    zeros[...] = jnp.zeros(zeros.shape, BF16)
    span = zeros.shape[0]
    clears = []
    for out in outs:
        for at in range(0, out.shape[0], span):
            here = min(span, out.shape[0] - at)
            clears.append(
                pltpu.make_async_copy(zeros.at[pl.ds(0, here)], out.at[pl.ds(at, here)], zero_sems.at[len(clears)])
            )

    nears = compact(nl, near_list, near_pairs)

    def fetch(i):
        return pltpu.make_async_copy(blocks.at[near_list[i]], held.at[i], block_sems.at[i])

    @pl.loop(0, nears)
    def _(i):
        fetch(i).start()

    for clear in clears:
        clear.start()
    fars = compact(fl, far_list, far_pairs)

    @pl.loop(0, tiles // 8)
    def _(i):
        for u in range(8):
            rank[i * 8 + u] = -1

    def slot(device, local):
        place = place_of(device ^ me, order_of(peers, spans[0][2]))
        for begin, length, z_first in spans[1:]:
            if z_first != spans[0][2]:
                here = (local >= begin) & (local < begin + length)
                place = jnp.where(here, place_of(device ^ me, order_of(peers, z_first)), place)
        return place * size + local - first

    def visit(at, found):
        fresh = rank[at] < 0

        @pl.when(fresh)
        def _():
            rank[at] = found
            tile[found] = at
            total[found] = jnp.zeros(total.shape[1:], F32)

        return found + jnp.where(fresh, 1, 0)

    def visit_far(i, found):
        p = far_list[i]
        return visit(slot(fd(p), fl(p)), found)

    def visit_near(i, found):
        p = near_list[i]
        return visit(slot(nd(p), nl(p)), found)

    found = lax.fori_loop(0, fars, visit_far, 0)
    found = lax.fori_loop(0, nears, visit_near, found)

    for load in loads:
        load.wait()

    @pl.loop(0, (fars + GROUP - 1) // GROUP)
    def _(g):
        for u in range(GROUP):
            p = far_list[g * GROUP + u]
            value = jnp.dot(basis_in[p], source[fs(p)], preferred_element_type=F32)
            coefficients[g * GROUP + u] = jnp.concatenate(pieces(value, 2), axis=0)

    @pl.loop(0, (fars + GROUP - 1) // GROUP)
    def _(g):
        parts = []
        for u in range(GROUP):
            i = g * GROUP + u
            p = far_list[i]
            basis = jnp.concatenate([basis_out[p], basis_out[p]], axis=0)
            at = jnp.where(i < fars, rank[slot(fd(p), jnp.where(i < fars, fl(p), first))], spare)
            parts.append((at, lax.dot_general(basis, coefficients[i], (((0,), (0,)), ((), ())), preferred_element_type=F32)))
        for at, part in parts:
            total[at] = total[at] + part

    rows = iota(source.shape[1:], 0)

    @pl.loop(0, (nears + GROUP - 1) // GROUP)
    def _(g):
        parts = []
        for u in range(GROUP):
            i = g * GROUP + u

            @pl.when(i < nears)
            def _():
                fetch(i).wait()

        for u in range(GROUP):
            i = g * GROUP + u
            p = near_list[i]
            chosen = jnp.where(rows < count(p), source[ns(p)].astype(F32), 0.0).astype(BF16)
            at = jnp.where(i < nears, rank[slot(nd(p), jnp.where(i < nears, nl(p), first))], spare)
            parts.append((at, jnp.dot(held[i], chosen, preferred_element_type=F32)))
        for at, part in parts:
            total[at] = total[at] + part

    for clear in clears:
        clear.wait()

    def store(i):
        place, local = tile[i] // size, tile[i] % size
        out = iter(outs)
        for begin, length, _ in spans:
            begin = begin - first
            for low, high in parts:
                to = next(out)
                here = (local >= begin) & (local < begin + length) & (place >= low) & (place < high)

                @pl.when(here)
                def _(to=to, low=low, begin=begin, length=length):
                    at = (place - low) * length + local - begin
                    pltpu.make_async_copy(staged.at[i], to.at[at], tile_sems.at[i]).start()

    @pl.loop(0, found)
    def _(i):
        staged[i] = total[i].astype(BF16)
        store(i)

    @pl.loop(0, found)
    def _(i):
        pltpu.make_async_copy(staged.at[i], outs[0].at[0], tile_sems.at[i]).wait()


def dense_sums(spans, peers, table, source, basis_in, basis_out, blocks):
    near_pairs, width, _ = blocks.shape
    far_pairs, rank, _ = basis_in.shape
    depth = source.shape[2]
    size = sum(length for _, length, _ in spans)
    most = min(peers * size, near_pairs + far_pairs)
    shapes, clears, span = [], 0, 16
    for _, length, _ in spans:
        for low, high in ranges(peers):
            tiles = (high - low) * length
            shapes.append(jax.ShapeDtypeStruct((tiles, width, depth), BF16))
            clears += -(-tiles // span)
    anywhere = pl.BlockSpec(memory_space=pl.ANY)
    outs = pl.pallas_call(
        functools.partial(sums_kernel, spans, peers, near_pairs, far_pairs),
        out_shape=tuple(shapes),
        in_specs=[smem()] + [pl.BlockSpec(memory_space=pltpu.HBM)] * 4,
        out_specs=(anywhere,) * len(shapes),
        scratch_shapes=[
            pltpu.VMEM((most + 1, width, depth), F32),
            pltpu.VMEM((near_pairs + GROUP, width, width), BF16),
            pltpu.VMEM((far_pairs + GROUP, 2 * rank, depth), BF16),
            pltpu.VMEM((span, width, depth), BF16),
            pltpu.VMEM((most, width, depth), BF16),
            pltpu.VMEM(source.shape, BF16),
            pltpu.VMEM(basis_in.shape, BF16),
            pltpu.VMEM(basis_out.shape, BF16),
            pltpu.SMEM((near_pairs + GROUP + 1,), I32),
            pltpu.SMEM((far_pairs + GROUP + 1,), I32),
            pltpu.SMEM((peers * size,), I32),
            pltpu.SMEM((most,), I32),
            pltpu.SemaphoreType.DMA((3,)),
            pltpu.SemaphoreType.DMA((near_pairs,)),
            pltpu.SemaphoreType.DMA((clears,)),
            pltpu.SemaphoreType.DMA((most,)),
        ],
        compiler_params=pltpu.CompilerParams(vmem_limit_bytes=VMEM_BYTES),
        cost_estimate=NO_COST,
        name="dense_sums",
    )(table, source, basis_in, basis_out, blocks)
    got = []
    for j, (_, length, _) in enumerate(spans):
        tile = (length, width, depth)
        leads = ((peers // 4,), (peers // 4,), (peers // 2,))
        got.append([out.reshape(lead + tile) for out, lead in zip(outs[3 * j : 3 * j + 3], leads)])
    return got


def pack_kernel(volume, stiffness, out):
    planes, cy, cz = volume.shape
    lanes = iota((cy, cz), 1)
    packed = jnp.zeros((cy, cz), F32)
    rows = iota((cy, cz), 0)

    def place(packed, column, at):
        return jnp.where(lanes == at, column, packed)

    for x in range(planes):
        here = volume[x]
        beside = jnp.where(rows == 0, 0.0, pltpu.roll(here, 1, 0))
        beside = beside + jnp.where(rows == cy - 1, 0.0, pltpu.roll(here, cy - 1, 0))
        if x > 0:
            beside = beside + volume[x - 1]
        if x < planes - 1:
            beside = beside + volume[x + 1]
        face = (6.0 + stiffness[x]) * here - beside
        column = face[:, 0:1] - here[:, 1:2]
        packed = place(packed, column, x)
    packed = place(packed, volume[0][:, 0:1], planes)
    packed = place(packed, volume[planes - 1][:, 0:1], planes + 1)
    packed = packed.T[: out.shape[1]]
    for n in range(out.shape[0]):
        out[n] = packed


def pack_face(peers, volume, stiffness):
    planes, cy, cz = volume.shape
    return pl.pallas_call(
        pack_kernel,
        out_shape=jax.ShapeDtypeStruct((peers, -(-(planes + 2) // 8) * 8, cy), F32),
        in_specs=[vmem()] * 2,
        out_specs=vmem(),
        compiler_params=pltpu.CompilerParams(vmem_limit_bytes=VMEM_BYTES),
        cost_estimate=NO_COST,
        name="pack_face",
    )(volume, stiffness)


def stencil_kernel(volume, stiffness, before, after, out):
    planes, cy, cz = volume.shape
    rows = iota((cy, cz), 0)
    lanes = iota((cy, cz), 1)
    for x in range(planes):
        here = volume[x]
        beside = (volume[x + 1] if x < planes - 1 else after[0]) + (volume[x - 1] if x > 0 else before[0])
        beside = beside + jnp.where(rows == cy - 1, 0.0, pltpu.roll(here, cy - 1, 0))
        beside = beside + jnp.where(rows == 0, 0.0, pltpu.roll(here, 1, 0))
        beside = beside + jnp.where(lanes == cz - 1, 0.0, pltpu.roll(here, cz - 1, 1))
        beside = beside + jnp.where(lanes == 0, 0.0, pltpu.roll(here, 1, 1))
        out[x] = (6.0 + stiffness[x]) * here - beside


def stencil(volume, stiffness, before, after):
    return pl.pallas_call(
        stencil_kernel,
        out_shape=jax.ShapeDtypeStruct(volume.shape, F32),
        in_specs=[vmem()] * 4,
        out_specs=vmem(),
        compiler_params=pltpu.CompilerParams(vmem_limit_bytes=VMEM_BYTES),
        cost_estimate=NO_COST,
        name="stencil",
    )(volume, stiffness, before, after)


def trace_kernel(
    ns, target, count, packs, places, near_blocks, basis_in, basis_out, far_source, far_target,
    traces, images, face,
):
    peers, _, cy = packs.shape
    nx = face.shape[0]
    planes = nx // peers
    clusters, width = places.shape
    rows8 = iota((planes, cy), 0)
    for n in range(peers):
        part = packs[n, 0:planes, :]
        if n > 0:
            part = part - jnp.where(rows8 == 0, packs[n - 1, planes + 1 : planes + 2, :], 0.0)
        if n < peers - 1:
            part = part - jnp.where(rows8 == planes - 1, packs[n + 1, planes : planes + 1, :], 0.0)
        face[n * planes : (n + 1) * planes, :] = part
    turned = jnp.concatenate(pieces(face[...].T, 3), axis=0)
    x_rows = iota((nx, width), 0)
    y_rows = iota((cy, width), 0)
    shift = cy.bit_length() - 1

    @pl.loop(0, clusters, unroll=4)
    def _(c):
        place = places[pl.ds(c, 1), :]
        picks = jnp.where(x_rows == (place >> shift), 1.0, 0.0).astype(BF16)
        columns = jnp.dot(turned, picks, preferred_element_type=F32)
        columns = columns[:cy] + columns[cy : 2 * cy] + columns[2 * cy :]
        found = jnp.where(y_rows == (place & (cy - 1)), columns, 0.0)
        traces[pl.ds(c, 1), :] = jnp.sum(found, axis=0, keepdims=True)

    contract = (((1,), (1,)), ((), ()))
    stacked = jnp.concatenate(pieces(traces[...], 2), axis=0)
    coefficients = lax.dot_general(stacked, basis_in[...], contract, preferred_element_type=F32)
    coefficients = coefficients[:clusters] + coefficients[clusters:]
    pairs_k = coefficients.shape[1]
    coefficients = jnp.where(iota((clusters, pairs_k), 0) == far_source[...], coefficients, 0.0)
    coefficients = jnp.sum(coefficients, axis=0, keepdims=True)
    block = 128

    @pl.loop(0, images.shape[0] // block)
    def _(b):
        base = pl.multiple_of(b * block, block)
        spread = jnp.where(iota((block, pairs_k), 0) + base == far_target[...], coefficients, 0.0)
        image = jnp.zeros((block, width), F32)
        for part in pieces(spread, 2):
            image = image + jnp.dot(part, basis_out[...], preferred_element_type=F32)
        images[pl.ds(base, block), :] = image

    lanes = iota((8, width), 1)
    rows = iota((8, width), 0)

    @pl.loop(0, near_blocks.shape[0] // GROUP)
    def _(g):
        parts = []
        for u in range(GROUP):
            p = g * GROUP + u
            at = target[p]
            trace = traces[pl.ds(ns[p], 1), :]
            placed = jnp.where((rows == (at & 7)) & (lanes < count[p]), trace, 0.0)
            both = jnp.concatenate(pieces(placed, 2), axis=0)
            image = lax.dot_general(both, near_blocks[p], contract, preferred_element_type=F32)
            parts.append((pl.multiple_of((at >> 3) * 8, 8), image[:8] + image[8:]))
        for base, image in parts:
            images[pl.ds(base, 8), :] = images[pl.ds(base, 8), :] + image


def trace_images(peers, nx, ns, target, count, packs, places, near_blocks, basis_in, basis_out, far_source, far_target):
    clusters, width = places.shape
    pairs, rank, _ = basis_in.shape
    return pl.pallas_call(
        trace_kernel,
        out_shape=(
            jax.ShapeDtypeStruct((clusters, width), F32),
            jax.ShapeDtypeStruct((peers * clusters, width), F32),
        ),
        in_specs=[smem()] * 3 + [vmem()] * 7,
        out_specs=(vmem(), vmem()),
        scratch_shapes=[pltpu.VMEM((nx, packs.shape[2]), F32)],
        compiler_params=pltpu.CompilerParams(vmem_limit_bytes=VMEM_BYTES),
        cost_estimate=NO_COST,
        name="trace_images",
    )(
        ns, target, count, packs, places, near_blocks,
        basis_in.reshape(pairs * rank, width), basis_out.reshape(pairs * rank, width),
        jnp.repeat(far_source, rank)[None, :], jnp.repeat(far_target, rank)[None, :],
    )


def sum_kernel(groups, *refs):
    outs = refs[len(refs) - len(groups) :]
    for out, group in zip(outs, groups):
        total = None
        for operand, index in group:
            term = refs[operand][index].astype(F32)
            total = term if total is None else total + term
        out[...] = total.astype(out.dtype)


def tile_sums(grid, groups, operands, outputs, aliases={}):
    return pl.pallas_call(
        functools.partial(sum_kernel, groups),
        grid=(grid,),
        out_shape=tuple(shape for shape, _, _ in outputs),
        in_specs=[pl.BlockSpec(block, index) for _, block, index in operands],
        out_specs=tuple(pl.BlockSpec(block, index) for _, block, index in outputs),
        input_output_aliases=aliases,
        compiler_params=pltpu.CompilerParams(vmem_limit_bytes=VMEM_BYTES),
        cost_estimate=NO_COST,
        name="tile_sums",
    )(*[array for array, _, _ in operands])


def block_of(size, most):
    return max(d for d in range(1, max(1, min(size, most)) + 1) if size % d == 0)


def half_sum(keep, other):
    places, tile = other.shape[0], other.shape[1:]
    step = max(1, places // 2)
    zeros = (0,) * len(tile)
    block = (step,) + tile
    return tile_sums(
        places // step, [[(0, ...), (1, ...)]],
        [(keep, block, lambda i: (places // step + i,) + zeros), (other, block, lambda i: (i,) + zeros)],
        [(jax.ShapeDtypeStruct(other.shape, BF16), block, lambda i: (i,) + zeros)],
    )[0]


def later_sum(places, *terms):
    size, width, depth = terms[0].shape[1:]
    step = block_of(size, 10 // places)
    block = (places, step, width, depth)
    return tile_sums(
        size // step, [[(i, ...) for i in range(len(terms))]],
        [(term, block, lambda i: (1, i, 0, 0)) for term in terms],
        [(jax.ShapeDtypeStruct((places, size, width, depth), BF16), block, lambda i: (0, i, 0, 0))],
    )[0]


def result(first, out, *terms):
    size, width, depth = terms[0].shape[1:]
    step = block_of(size, 5)
    while first % step:
        step = block_of(size, step - 1)
    tile = (step, width, depth)
    here = (out, tile, lambda i: (first // step + i, 0, 0))
    operands = [here] + [(term, (None,) + tile, lambda i: (0, i, 0, 0)) for term in terms]
    return tile_sums(
        size // step, [[(i, ...) for i in range(len(operands))]], operands,
        [(jax.ShapeDtypeStruct(out.shape, F32),) + here[1:]], {0: 0},
    )[0]


def swap(value, bit):
    peers = lax.axis_size("clus")
    return lax.ppermute(value, "clus", [(i, i ^ bit) for i in range(peers)])


class Sent:
    def __init__(self, value):
        self.value = value


class Order:
    def __init__(self, token):
        self.token = token
        self.sent = []

    def send(self, value):
        self.sent.append(Sent(value))
        return self.sent[-1]

    def wait(self):
        values = self(lambda *a: a, *[sent.value for sent in self.sent])
        for sent, value in zip(self.sent, values):
            sent.value = value
        self.sent = []

    def __call__(self, act, *args):
        args, _ = lax.optimization_barrier((args, self.token))
        out = act(*args)
        self.token = jax.tree.leaves(out)[0]
        return out


def body(
    adjoint_volume,
    stiffness,
    boundary_source,
    trace_gain,
    trace_map,
    near_blocks,
    near_source,
    near_target_dev,
    near_target_local,
    close_block_column_count,
    far_basis_in,
    far_basis_out,
    far_source,
    far_target_dev,
    far_target_local,
):
    peers = lax.axis_size("clus")
    clusters = boundary_source.shape[0]
    planes = adjoint_volume.shape[0]
    near_owner = near_target_dev.reshape(-1)
    far_owner = far_target_dev.reshape(-1)
    table = jnp.concatenate([
        near_source, near_owner, near_target_local, close_block_column_count,
        far_source, far_owner, far_target_local,
    ])
    near_target = near_owner * clusters + near_target_local
    far_target = far_owner * clusters + far_target_local
    order = Order(table)
    got = {}

    def sums():
        for call in range(1 + max(call for _, _, call in PLAN)):
            chunks = [j for j, plan in enumerate(PLAN) if plan[2] == call]
            pairs = order(
                lambda *a: dense_sums([spans[j] for j in chunks], peers, *a),
                table, boundary_source, far_basis_in, far_basis_out, near_blocks,
            )
            for j, pair in zip(chunks, pairs):
                got[j] = pair
            yield

    def chunk(j):
        same, other, keep = got[j]
        bits = order_of(peers, PLAN[j][1])[1:]
        other, same = order.send(swap(other, 1)), order.send(swap(same, 1))
        yield
        sent = [order.send(swap(order(half_sum, keep, other.value), bits[0]))]
        yield
        places = peers // 8
        for step, bit in enumerate(bits[1:]):
            terms = [keep, same.value] + [each.value for each in sent]
            sent.append(order.send(swap(order(functools.partial(later_sum, places), *terms), bit)))
            if step == 0 or places == 1:
                yield
            places //= 2
        terms = [keep, same.value] + [each.value for each in sent]
        got["out"] = order(functools.partial(result, spans[j][0]), got["out"], *terms)
        yield

    def exchange(value):
        return order.send(lax.all_to_all(value, "clus", split_axis=0, concat_axis=0, tiled=True))

    def face():
        packs = exchange(order(functools.partial(pack_face, peers), adjoint_volume, stiffness))
        yield
        traces, images = order(
            lambda packs, near: trace_images(
                peers, planes * peers, near_source, near_target, close_block_column_count,
                packs, trace_map, near, far_basis_in, far_basis_out, far_source, far_target,
            ),
            packs.value, near_blocks,
        )
        images = exchange(images.reshape((peers, clusters) + images.shape[1:]))
        yield
        got["out"] = order(
            lambda out, g, t, i: out + (t + jnp.sum(i, axis=0))[:, :, None] * g[None, None, :],
            got["out"], trace_gain, traces, images.value,
        )
        yield

    def base():
        got["out"] = order(lambda s: s.astype(F32), boundary_source)
        yield

    def volume():
        ends = peers - 1
        tail, head = order(lambda v: (v[planes - 1 :], v[:1]), adjoint_volume)
        before = order.send(lax.ppermute(tail, "clus", [(i, i + 1) for i in range(ends)]))
        after = order.send(lax.ppermute(head, "clus", [(i + 1, i) for i in range(ends)]))
        yield
        got["volume"] = order(stencil, adjoint_volume, stiffness, before.value, after.value)
        yield

    spans, first = [], 0
    for share, z_first, _ in PLAN:
        spans.append((first, share * clusters // 16, z_first))
        first += spans[-1][1]
    runs = {"s": sums(), "f": face(), "v": volume(), "b": base()}
    runs.update((str(j), chunk(j)) for j in range(len(PLAN)))
    for name in SEQUENCE:
        if name == "w":
            order.wait()
        else:
            next(runs[name])
    return got["volume"], got["out"]


def solution(mesh):
    whole = ("groups", "clus")
    one, two, three = P(whole), P(whole, None), P(whole, None, None)
    return jax.shard_map(
        body,
        mesh=mesh,
        in_specs=(three, three, three, P(), two, three, one, two, one, one, three, three, one, two, one),
        out_specs=(three, three),
        check_vma=False,
    )
```

```python
import functools

import jax
import jax.numpy as jnp
from jax import lax
from jax.experimental import pallas as pl
from jax.experimental.pallas import tpu as pltpu
from jax.sharding import PartitionSpec as P

F32 = jnp.float32
BF16 = jnp.bfloat16
I32 = jnp.int32
MIB = 1 << 20
VMEM_BYTES = 60 * MIB
NO_COST = pl.CostEstimate(flops=1, bytes_accessed=1, transcendentals=0)

PLAN = ((5, False, 0), (5, True, 0), (4, False, 1), (2, False, 1))

SEQUENCE = tuple("s0101s23lfbw20l1w203lfw1320vw3f12vw3")


def smem():
    return pl.BlockSpec(memory_space=pltpu.SMEM)


def vmem():
    return pl.BlockSpec(memory_space=pltpu.VMEM)


def iota(shape, dim):
    return lax.broadcasted_iota(I32, shape, dim)


def pieces(value, count):
    out = []
    for _ in range(count):
        part = value.astype(BF16)
        out.append(part)
        value = value - part.astype(F32)
    return out


GROUP = 4


def order_of(peers, z_first):
    z = []
    bit = 4
    while bit < peers:
        z.append(bit)
        bit *= 2
    return [1] + z + [2] if z_first else [1, 2] + z


def place_of(apart, bits):
    place = 0
    for bit in bits:
        place = place * 2 + jnp.where((apart & bit) != 0, 1, 0)
    return place


def ranges(peers):
    return ((peers // 2, 3 * peers // 4), (3 * peers // 4, peers), (0, peers // 2))


def sums_kernel(spans, peers, near_pairs, far_pairs, table, far_source, far_in, far_out, blocks, *refs):
    parts = ranges(peers)
    outs = refs[: len(spans) * len(parts)]
    (total, held, coefficients, zeros, staged, source, basis_in, basis_out, near_list, far_list, rank, tile,
     load_sems, block_sems, zero_sems, tile_sems) = refs[len(outs) :]
    loads = [
        pltpu.make_async_copy(whole, part, load_sems.at[i])
        for i, (whole, part) in enumerate(((far_source, source), (far_in, basis_in), (far_out, basis_out)))
    ]
    for load in loads:
        load.start()
    me = lax.axis_index("clus")
    half = peers // 2
    first = spans[0][0]
    size = sum(length for _, length, _ in spans)
    tiles = peers * size
    ns, nd, nl, count, fs, fd, fl = [
        (lambda at: lambda p: table[at + p])(at)
        for at in (0, near_pairs, 2 * near_pairs, 3 * near_pairs, 4 * near_pairs, 4 * near_pairs + far_pairs, 4 * near_pairs + 2 * far_pairs)
    ]
    spare = total.shape[0] - 1

    def compact(local, listing, pairs):
        def step(p, found):
            at = local(p)
            listing[found] = p
            return found + jnp.where((at >= first) & (at < first + size), 1, 0)

        found = lax.fori_loop(0, pairs, step, 0, unroll=8)
        for u in range(GROUP):
            listing[found + u] = 0
        return found

    zeros[...] = jnp.zeros(zeros.shape, BF16)
    span = zeros.shape[0]
    clears = []
    for out in outs:
        for at in range(0, out.shape[0], span):
            here = min(span, out.shape[0] - at)
            clears.append(
                pltpu.make_async_copy(zeros.at[pl.ds(0, here)], out.at[pl.ds(at, here)], zero_sems.at[len(clears)])
            )

    nears = compact(nl, near_list, near_pairs)

    def fetch(i):
        return pltpu.make_async_copy(blocks.at[near_list[i]], held.at[i], block_sems.at[i])

    @pl.loop(0, nears)
    def _(i):
        fetch(i).start()

    for clear in clears:
        clear.start()
    fars = compact(fl, far_list, far_pairs)

    @pl.loop(0, tiles // 8)
    def _(i):
        for u in range(8):
            rank[i * 8 + u] = -1

    def slot(device, local):
        place = place_of(device ^ me, order_of(peers, spans[0][2]))
        for begin, length, z_first in spans[1:]:
            if z_first != spans[0][2]:
                here = (local >= begin) & (local < begin + length)
                place = jnp.where(here, place_of(device ^ me, order_of(peers, z_first)), place)
        return place * size + local - first

    def visit(at, found):
        fresh = rank[at] < 0

        @pl.when(fresh)
        def _():
            rank[at] = found
            tile[found] = at
            total[found] = jnp.zeros(total.shape[1:], F32)

        return found + jnp.where(fresh, 1, 0)

    def visit_far(i, found):
        p = far_list[i]
        return visit(slot(fd(p), fl(p)), found)

    def visit_near(i, found):
        p = near_list[i]
        return visit(slot(nd(p), nl(p)), found)

    found = lax.fori_loop(0, fars, visit_far, 0)
    found = lax.fori_loop(0, nears, visit_near, found)

    for load in loads:
        load.wait()

    @pl.loop(0, (fars + GROUP - 1) // GROUP)
    def _(g):
        for u in range(GROUP):
            p = far_list[g * GROUP + u]
            value = jnp.dot(basis_in[p], source[fs(p)], preferred_element_type=F32)
            coefficients[g * GROUP + u] = jnp.concatenate(pieces(value, 2), axis=0)

    @pl.loop(0, (fars + GROUP - 1) // GROUP)
    def _(g):
        parts = []
        for u in range(GROUP):
            i = g * GROUP + u
            p = far_list[i]
            basis = jnp.concatenate([basis_out[p], basis_out[p]], axis=0)
            at = jnp.where(i < fars, rank[slot(fd(p), jnp.where(i < fars, fl(p), first))], spare)
            parts.append((at, lax.dot_general(basis, coefficients[i], (((0,), (0,)), ((), ())), preferred_element_type=F32)))
        for at, part in parts:
            total[at] = total[at] + part

    rows = iota(source.shape[1:], 0)

    @pl.loop(0, (nears + GROUP - 1) // GROUP)
    def _(g):
        parts = []
        for u in range(GROUP):
            i = g * GROUP + u

            @pl.when(i < nears)
            def _():
                fetch(i).wait()

        for u in range(GROUP):
            i = g * GROUP + u
            p = near_list[i]
            chosen = jnp.where(rows < count(p), source[ns(p)].astype(F32), 0.0).astype(BF16)
            at = jnp.where(i < nears, rank[slot(nd(p), jnp.where(i < nears, nl(p), first))], spare)
            parts.append((at, jnp.dot(held[i], chosen, preferred_element_type=F32)))
        for at, part in parts:
            total[at] = total[at] + part

    for clear in clears:
        clear.wait()

    def store(i):
        place, local = tile[i] // size, tile[i] % size
        out = iter(outs)
        for begin, length, _ in spans:
            begin = begin - first
            for low, high in parts:
                to = next(out)
                here = (local >= begin) & (local < begin + length) & (place >= low) & (place < high)

                @pl.when(here)
                def _(to=to, low=low, begin=begin, length=length):
                    at = (place - low) * length + local - begin
                    pltpu.make_async_copy(staged.at[i], to.at[at], tile_sems.at[i]).start()

    @pl.loop(0, found)
    def _(i):
        staged[i] = total[i].astype(BF16)
        store(i)

    @pl.loop(0, found)
    def _(i):
        pltpu.make_async_copy(staged.at[i], outs[0].at[0], tile_sems.at[i]).wait()


def dense_sums(spans, peers, table, source, basis_in, basis_out, blocks):
    near_pairs, width, _ = blocks.shape
    far_pairs, rank, _ = basis_in.shape
    depth = source.shape[2]
    size = sum(length for _, length, _ in spans)
    most = min(peers * size, near_pairs + far_pairs)
    shapes, clears, span = [], 0, 16
    for _, length, _ in spans:
        for low, high in ranges(peers):
            tiles = (high - low) * length
            shapes.append(jax.ShapeDtypeStruct((tiles, width, depth), BF16))
            clears += -(-tiles // span)
    anywhere = pl.BlockSpec(memory_space=pl.ANY)
    outs = pl.pallas_call(
        functools.partial(sums_kernel, spans, peers, near_pairs, far_pairs),
        out_shape=tuple(shapes),
        in_specs=[smem()] + [pl.BlockSpec(memory_space=pltpu.HBM)] * 4,
        out_specs=(anywhere,) * len(shapes),
        scratch_shapes=[
            pltpu.VMEM((most + 1, width, depth), F32),
            pltpu.VMEM((near_pairs + GROUP, width, width), BF16),
            pltpu.VMEM((far_pairs + GROUP, 2 * rank, depth), BF16),
            pltpu.VMEM((span, width, depth), BF16),
            pltpu.VMEM((most, width, depth), BF16),
            pltpu.VMEM(source.shape, BF16),
            pltpu.VMEM(basis_in.shape, BF16),
            pltpu.VMEM(basis_out.shape, BF16),
            pltpu.SMEM((near_pairs + GROUP + 1,), I32),
            pltpu.SMEM((far_pairs + GROUP + 1,), I32),
            pltpu.SMEM((peers * size,), I32),
            pltpu.SMEM((most,), I32),
            pltpu.SemaphoreType.DMA((3,)),
            pltpu.SemaphoreType.DMA((near_pairs,)),
            pltpu.SemaphoreType.DMA((clears,)),
            pltpu.SemaphoreType.DMA((most,)),
        ],
        compiler_params=pltpu.CompilerParams(vmem_limit_bytes=VMEM_BYTES),
        cost_estimate=NO_COST,
        name="dense_sums",
    )(table, source, basis_in, basis_out, blocks)
    got = []
    for j, (_, length, _) in enumerate(spans):
        tile = (length, width, depth)
        leads = ((peers // 4,), (peers // 4,), (peers // 2,))
        got.append([out.reshape(lead + tile) for out, lead in zip(outs[3 * j : 3 * j + 3], leads)])
    return got


def pack_kernel(volume, stiffness, out):
    planes, cy, cz = volume.shape
    lanes = iota((cy, cz), 1)
    packed = jnp.zeros((cy, cz), F32)
    rows = iota((cy, cz), 0)

    def place(packed, column, at):
        return jnp.where(lanes == at, column, packed)

    for x in range(planes):
        here = volume[x]
        beside = jnp.where(rows == 0, 0.0, pltpu.roll(here, 1, 0))
        beside = beside + jnp.where(rows == cy - 1, 0.0, pltpu.roll(here, cy - 1, 0))
        if x > 0:
            beside = beside + volume[x - 1]
        if x < planes - 1:
            beside = beside + volume[x + 1]
        face = (6.0 + stiffness[x]) * here - beside
        column = face[:, 0:1] - here[:, 1:2]
        packed = place(packed, column, x)
    packed = place(packed, volume[0][:, 0:1], planes)
    packed = place(packed, volume[planes - 1][:, 0:1], planes + 1)
    packed = packed.T[: out.shape[1]]
    for n in range(out.shape[0]):
        out[n] = packed


def pack_face(peers, volume, stiffness):
    planes, cy, cz = volume.shape
    return pl.pallas_call(
        pack_kernel,
        out_shape=jax.ShapeDtypeStruct((peers, -(-(planes + 2) // 8) * 8, cy), F32),
        in_specs=[vmem()] * 2,
        out_specs=vmem(),
        compiler_params=pltpu.CompilerParams(vmem_limit_bytes=VMEM_BYTES),
        cost_estimate=NO_COST,
        name="pack_face",
    )(volume, stiffness)


def stencil_kernel(volume, stiffness, before, after, out):
    planes, cy, cz = volume.shape
    rows = iota((cy, cz), 0)
    lanes = iota((cy, cz), 1)
    for x in range(planes):
        here = volume[x]
        beside = (volume[x + 1] if x < planes - 1 else after[0]) + (volume[x - 1] if x > 0 else before[0])
        beside = beside + jnp.where(rows == cy - 1, 0.0, pltpu.roll(here, cy - 1, 0))
        beside = beside + jnp.where(rows == 0, 0.0, pltpu.roll(here, 1, 0))
        beside = beside + jnp.where(lanes == cz - 1, 0.0, pltpu.roll(here, cz - 1, 1))
        beside = beside + jnp.where(lanes == 0, 0.0, pltpu.roll(here, 1, 1))
        out[x] = (6.0 + stiffness[x]) * here - beside


def stencil(volume, stiffness, before, after):
    return pl.pallas_call(
        stencil_kernel,
        out_shape=jax.ShapeDtypeStruct(volume.shape, F32),
        in_specs=[vmem()] * 4,
        out_specs=vmem(),
        compiler_params=pltpu.CompilerParams(vmem_limit_bytes=VMEM_BYTES),
        cost_estimate=NO_COST,
        name="stencil",
    )(volume, stiffness, before, after)


def trace_kernel(
    ns, target, count, packs, places, near_blocks, basis_in, basis_out, far_source, far_target,
    traces, images, face,
):
    peers, _, cy = packs.shape
    nx = face.shape[0]
    planes = nx // peers
    clusters, width = places.shape
    rows8 = iota((planes, cy), 0)
    for n in range(peers):
        part = packs[n, 0:planes, :]
        if n > 0:
            part = part - jnp.where(rows8 == 0, packs[n - 1, planes + 1 : planes + 2, :], 0.0)
        if n < peers - 1:
            part = part - jnp.where(rows8 == planes - 1, packs[n + 1, planes : planes + 1, :], 0.0)
        face[n * planes : (n + 1) * planes, :] = part
    turned = jnp.concatenate(pieces(face[...].T, 3), axis=0)
    x_rows = iota((nx, width), 0)
    y_rows = iota((cy, width), 0)
    shift = cy.bit_length() - 1

    @pl.loop(0, clusters, unroll=4)
    def _(c):
        place = places[pl.ds(c, 1), :]
        picks = jnp.where(x_rows == (place >> shift), 1.0, 0.0).astype(BF16)
        columns = jnp.dot(turned, picks, preferred_element_type=F32)
        columns = columns[:cy] + columns[cy : 2 * cy] + columns[2 * cy :]
        found = jnp.where(y_rows == (place & (cy - 1)), columns, 0.0)
        traces[pl.ds(c, 1), :] = jnp.sum(found, axis=0, keepdims=True)

    contract = (((1,), (1,)), ((), ()))
    stacked = jnp.concatenate(pieces(traces[...], 2), axis=0)
    coefficients = lax.dot_general(stacked, basis_in[...], contract, preferred_element_type=F32)
    coefficients = coefficients[:clusters] + coefficients[clusters:]
    pairs_k = coefficients.shape[1]
    coefficients = jnp.where(iota((clusters, pairs_k), 0) == far_source[...], coefficients, 0.0)
    coefficients = jnp.sum(coefficients, axis=0, keepdims=True)
    block = 128

    @pl.loop(0, images.shape[0] // block)
    def _(b):
        base = pl.multiple_of(b * block, block)
        spread = jnp.where(iota((block, pairs_k), 0) + base == far_target[...], coefficients, 0.0)
        image = jnp.zeros((block, width), F32)
        for part in pieces(spread, 2):
            image = image + jnp.dot(part, basis_out[...], preferred_element_type=F32)
        images[pl.ds(base, block), :] = image

    lanes = iota((8, width), 1)
    rows = iota((8, width), 0)

    @pl.loop(0, near_blocks.shape[0] // GROUP)
    def _(g):
        parts = []
        for u in range(GROUP):
            p = g * GROUP + u
            at = target[p]
            trace = traces[pl.ds(ns[p], 1), :]
            placed = jnp.where((rows == (at & 7)) & (lanes < count[p]), trace, 0.0)
            both = jnp.concatenate(pieces(placed, 2), axis=0)
            image = lax.dot_general(both, near_blocks[p], contract, preferred_element_type=F32)
            parts.append((pl.multiple_of((at >> 3) * 8, 8), image[:8] + image[8:]))
        for base, image in parts:
            images[pl.ds(base, 8), :] = images[pl.ds(base, 8), :] + image


def trace_images(peers, nx, ns, target, count, packs, places, near_blocks, basis_in, basis_out, far_source, far_target):
    clusters, width = places.shape
    pairs, rank, _ = basis_in.shape
    return pl.pallas_call(
        trace_kernel,
        out_shape=(
            jax.ShapeDtypeStruct((clusters, width), F32),
            jax.ShapeDtypeStruct((peers * clusters, width), F32),
        ),
        in_specs=[smem()] * 3 + [vmem()] * 7,
        out_specs=(vmem(), vmem()),
        scratch_shapes=[pltpu.VMEM((nx, packs.shape[2]), F32)],
        compiler_params=pltpu.CompilerParams(vmem_limit_bytes=VMEM_BYTES),
        cost_estimate=NO_COST,
        name="trace_images",
    )(
        ns, target, count, packs, places, near_blocks,
        basis_in.reshape(pairs * rank, width), basis_out.reshape(pairs * rank, width),
        jnp.repeat(far_source, rank)[None, :], jnp.repeat(far_target, rank)[None, :],
    )


def sum_kernel(groups, *refs):
    outs = refs[len(refs) - len(groups) :]
    for out, group in zip(outs, groups):
        total = None
        for operand, index in group:
            term = refs[operand][index].astype(F32)
            total = term if total is None else total + term
        out[...] = total.astype(out.dtype)


def tile_sums(grid, groups, operands, outputs, aliases={}):
    return pl.pallas_call(
        functools.partial(sum_kernel, groups),
        grid=(grid,),
        out_shape=tuple(shape for shape, _, _ in outputs),
        in_specs=[pl.BlockSpec(block, index) for _, block, index in operands],
        out_specs=tuple(pl.BlockSpec(block, index) for _, block, index in outputs),
        input_output_aliases=aliases,
        compiler_params=pltpu.CompilerParams(vmem_limit_bytes=VMEM_BYTES),
        cost_estimate=NO_COST,
        name="tile_sums",
    )(*[array for array, _, _ in operands])


def block_of(size, most):
    return max(d for d in range(1, max(1, min(size, most)) + 1) if size % d == 0)


def half_sum(keep, other):
    places, tile = other.shape[0], other.shape[1:]
    step = max(1, places // 2)
    zeros = (0,) * len(tile)
    block = (step,) + tile
    return tile_sums(
        places // step, [[(0, ...), (1, ...)]],
        [(keep, block, lambda i: (places // step + i,) + zeros), (other, block, lambda i: (i,) + zeros)],
        [(jax.ShapeDtypeStruct(other.shape, BF16), block, lambda i: (i,) + zeros)],
    )[0]


def later_sum(places, *terms):
    size, width, depth = terms[0].shape[1:]
    step = block_of(size, 10 // places)
    block = (places, step, width, depth)
    return tile_sums(
        size // step, [[(i, ...) for i in range(len(terms))]],
        [(term, block, lambda i: (1, i, 0, 0)) for term in terms],
        [(jax.ShapeDtypeStruct((places, size, width, depth), BF16), block, lambda i: (0, i, 0, 0))],
    )[0]


def result(first, out, *terms):
    size, width, depth = terms[0].shape[1:]
    step = block_of(size, 5)
    while first % step:
        step = block_of(size, step - 1)
    tile = (step, width, depth)
    here = (out, tile, lambda i: (first // step + i, 0, 0))
    operands = [here] + [(term, (None,) + tile, lambda i: (0, i, 0, 0)) for term in terms]
    return tile_sums(
        size // step, [[(i, ...) for i in range(len(operands))]], operands,
        [(jax.ShapeDtypeStruct(out.shape, F32),) + here[1:]], {0: 0},
    )[0]


def swap(value, bit):
    peers = lax.axis_size("clus")
    return lax.ppermute(value, "clus", [(i, i ^ bit) for i in range(peers)])


class Sent:
    def __init__(self, value):
        self.value = value


class Order:
    def __init__(self, token):
        self.token = token
        self.sent, self.later, self.late = [], [], False

    def send(self, value):
        sent = Sent(value)
        (self.later if self.late else self.sent).append(sent)
        return sent

    def wait(self):
        values = self(lambda *a: a, *[sent.value for sent in self.sent])
        for sent, value in zip(self.sent, values):
            sent.value = value
        self.sent, self.later = self.later, []

    def __call__(self, act, *args):
        args, _ = lax.optimization_barrier((args, self.token))
        out = act(*args)
        self.token = jax.tree.leaves(out)[0]
        return out


def body(
    adjoint_volume,
    stiffness,
    boundary_source,
    trace_gain,
    trace_map,
    near_blocks,
    near_source,
    near_target_dev,
    near_target_local,
    close_block_column_count,
    far_basis_in,
    far_basis_out,
    far_source,
    far_target_dev,
    far_target_local,
):
    peers = lax.axis_size("clus")
    clusters = boundary_source.shape[0]
    planes = adjoint_volume.shape[0]
    near_owner = near_target_dev.reshape(-1)
    far_owner = far_target_dev.reshape(-1)
    table = jnp.concatenate([
        near_source, near_owner, near_target_local, close_block_column_count,
        far_source, far_owner, far_target_local,
    ])
    near_target = near_owner * clusters + near_target_local
    far_target = far_owner * clusters + far_target_local
    order = Order(table)
    got = {}

    def sums():
        for call in range(1 + max(call for _, _, call in PLAN)):
            chunks = [j for j, plan in enumerate(PLAN) if plan[2] == call]
            pairs = order(
                lambda *a: dense_sums([spans[j] for j in chunks], peers, *a),
                table, boundary_source, far_basis_in, far_basis_out, near_blocks,
            )
            for j, pair in zip(chunks, pairs):
                got[j] = pair
            yield

    def chunk(j):
        same, other, keep = got[j]
        bits = order_of(peers, PLAN[j][1])[1:]
        other, same = order.send(swap(other, 1)), order.send(swap(same, 1))
        yield
        sent = [order.send(swap(order(half_sum, keep, other.value), bits[0]))]
        yield
        places = peers // 8
        for step, bit in enumerate(bits[1:]):
            terms = [keep, same.value] + [each.value for each in sent]
            sent.append(order.send(swap(order(functools.partial(later_sum, places), *terms), bit)))
            if step == 0 or places == 1:
                yield
            places //= 2
        terms = [keep, same.value] + [each.value for each in sent]
        got["out"] = order(functools.partial(result, spans[j][0]), got["out"], *terms)
        yield

    def exchange(value):
        return order.send(lax.all_to_all(value, "clus", split_axis=0, concat_axis=0, tiled=True))

    def face():
        packs = exchange(order(functools.partial(pack_face, peers), adjoint_volume, stiffness))
        yield
        traces, images = order(
            lambda packs, near: trace_images(
                peers, planes * peers, near_source, near_target, close_block_column_count,
                packs, trace_map, near, far_basis_in, far_basis_out, far_source, far_target,
            ),
            packs.value, near_blocks,
        )
        images = exchange(images.reshape((peers, clusters) + images.shape[1:]))
        yield
        got["out"] = order(
            lambda out, g, t, i: out + (t + jnp.sum(i, axis=0))[:, :, None] * g[None, None, :],
            got["out"], trace_gain, traces, images.value,
        )
        yield

    def base():
        got["out"] = order(lambda s: s.astype(F32), boundary_source)
        yield

    def volume():
        ends = peers - 1
        tail, head = order(lambda v: (v[planes - 1 :], v[:1]), adjoint_volume)
        before = order.send(lax.ppermute(tail, "clus", [(i, i + 1) for i in range(ends)]))
        after = order.send(lax.ppermute(head, "clus", [(i + 1, i) for i in range(ends)]))
        yield
        got["volume"] = order(stencil, adjoint_volume, stiffness, before.value, after.value)
        yield

    spans, first = [], 0
    for share, z_first, _ in PLAN:
        spans.append((first, share * clusters // 16, z_first))
        first += spans[-1][1]
    runs = {"s": sums(), "f": face(), "v": volume(), "b": base()}
    runs.update((str(j), chunk(j)) for j in range(len(PLAN)))
    for name in SEQUENCE:
        if name == "w":
            order.wait()
        elif name != "l":
            next(runs[name])
        order.late = name == "l"
    return got["volume"], got["out"]


def solution(mesh):
    whole = ("groups", "clus")
    one, two, three = P(whole), P(whole, None), P(whole, None, None)
    return jax.shard_map(
        body,
        mesh=mesh,
        in_specs=(three, three, three, P(), two, three, one, two, one, one, three, three, one, two, one),
        out_specs=(three, three),
        check_vma=False,
    )
```

```python
import functools
import math

import jax
import jax.numpy as jnp
from jax import lax
from jax.experimental import pallas as pl
from jax.experimental.pallas import tpu as pltpu
from jax.sharding import PartitionSpec as P

F32 = jnp.float32
BF16 = jnp.bfloat16
I32 = jnp.int32
MIB = 1 << 20
VMEM_BYTES = 60 * MIB
NO_COST = pl.CostEstimate(flops=1, bytes_accessed=1, transcendentals=0)

PLAN = ((5, False, 0), (5, True, 0), (4, False, 1), (2, False, 1))

SEQUENCE = tuple("s0101s23lfbw20l1w203lflvw1320vw3f12w3")


def smem():
    return pl.BlockSpec(memory_space=pltpu.SMEM)


def vmem():
    return pl.BlockSpec(memory_space=pltpu.VMEM)


def iota(shape, dim):
    return lax.broadcasted_iota(I32, shape, dim)


def pieces(value, count):
    out = []
    for _ in range(count):
        part = value.astype(BF16)
        out.append(part)
        value = value - part.astype(F32)
    return out


GROUP = 8


def order_of(peers, z_first):
    z = []
    bit = 4
    while bit < peers:
        z.append(bit)
        bit *= 2
    return [1] + z + [2] if z_first else [1, 2] + z


def place_of(apart, bits):
    place = 0
    for bit in bits:
        place = place * 2 + jnp.where((apart & bit) != 0, 1, 0)
    return place


def ranges(peers):
    return ((peers // 2, 3 * peers // 4), (3 * peers // 4, peers), (0, peers // 2))


def sums_kernel(spans, peers, near_pairs, far_pairs, table, far_source, far_in, far_out, blocks, *refs):
    parts = ranges(peers)
    outs = refs[: len(spans) * len(parts)]
    (total, held, coefficients, zeros, staged, source, basis_in, basis_out, near_list, far_list, rank, tile,
     load_sems, block_sems, zero_sems, tile_sems) = refs[len(outs) :]
    loads = [
        pltpu.make_async_copy(whole, part, load_sems.at[i])
        for i, (whole, part) in enumerate(((far_source, source), (far_in, basis_in), (far_out, basis_out)))
    ]
    for load in loads:
        load.start()
    me = lax.axis_index("clus")
    half = peers // 2
    first = spans[0][0]
    size = sum(length for _, length, _ in spans)
    tiles = peers * size
    ns, nd, nl, count, fs, fd, fl = [
        (lambda at: lambda p: table[at + p])(at)
        for at in (0, near_pairs, 2 * near_pairs, 3 * near_pairs, 4 * near_pairs, 4 * near_pairs + far_pairs, 4 * near_pairs + 2 * far_pairs)
    ]
    spare = total.shape[0] - 1

    def compact(local, listing, pairs):
        def step(p, found):
            at = local(p)
            listing[found] = p
            return found + jnp.where((at >= first) & (at < first + size), 1, 0)

        found = lax.fori_loop(0, pairs, step, 0, unroll=8)
        for u in range(GROUP):
            listing[found + u] = 0
        return found

    zeros[...] = jnp.zeros(zeros.shape, BF16)
    span = zeros.shape[0]
    clears = []
    for out in outs:
        for at in range(0, out.shape[0], span):
            here = min(span, out.shape[0] - at)
            clears.append(
                pltpu.make_async_copy(zeros.at[pl.ds(0, here)], out.at[pl.ds(at, here)], zero_sems.at[len(clears)])
            )

    nears = compact(nl, near_list, near_pairs)

    def fetch(i):
        return pltpu.make_async_copy(blocks.at[near_list[i]], held.at[i], block_sems.at[i])

    @pl.loop(0, nears)
    def _(i):
        fetch(i).start()

    for clear in clears:
        clear.start()
    fars = compact(fl, far_list, far_pairs)

    @pl.loop(0, tiles // 8)
    def _(i):
        for u in range(8):
            rank[i * 8 + u] = -1

    def slot(device, local):
        place = place_of(device ^ me, order_of(peers, spans[0][2]))
        for begin, length, z_first in spans[1:]:
            if z_first != spans[0][2]:
                here = (local >= begin) & (local < begin + length)
                place = jnp.where(here, place_of(device ^ me, order_of(peers, z_first)), place)
        return place * size + local - first

    def visit(at, found):
        fresh = rank[at] < 0

        @pl.when(fresh)
        def _():
            rank[at] = found
            tile[found] = at
            total[found] = jnp.zeros(total.shape[1:], F32)

        return found + jnp.where(fresh, 1, 0)

    def visit_far(i, found):
        p = far_list[i]
        return visit(slot(fd(p), fl(p)), found)

    def visit_near(i, found):
        p = near_list[i]
        return visit(slot(nd(p), nl(p)), found)

    found = lax.fori_loop(0, fars, visit_far, 0)
    found = lax.fori_loop(0, nears, visit_near, found)

    for load in loads:
        load.wait()

    @pl.loop(0, (fars + GROUP - 1) // GROUP)
    def _(g):
        for u in range(GROUP):
            p = far_list[g * GROUP + u]
            value = jnp.dot(basis_in[p], source[fs(p)], preferred_element_type=F32)
            coefficients[g * GROUP + u] = jnp.concatenate(pieces(value, 2), axis=0)

    @pl.loop(0, (fars + GROUP - 1) // GROUP)
    def _(g):
        parts = []
        for u in range(GROUP):
            i = g * GROUP + u
            p = far_list[i]
            basis = jnp.concatenate([basis_out[p], basis_out[p]], axis=0)
            at = jnp.where(i < fars, rank[slot(fd(p), jnp.where(i < fars, fl(p), first))], spare)
            parts.append((at, lax.dot_general(basis, coefficients[i], (((0,), (0,)), ((), ())), preferred_element_type=F32)))
        for at, part in parts:
            total[at] = total[at] + part

    rows = iota(source.shape[1:], 0)

    @pl.loop(0, (nears + GROUP - 1) // GROUP)
    def _(g):
        parts = []
        for u in range(GROUP):
            i = g * GROUP + u

            @pl.when(i < nears)
            def _():
                fetch(i).wait()

        for u in range(GROUP):
            i = g * GROUP + u
            p = near_list[i]
            chosen = jnp.where(rows < count(p), source[ns(p)].astype(F32), 0.0).astype(BF16)
            at = jnp.where(i < nears, rank[slot(nd(p), jnp.where(i < nears, nl(p), first))], spare)
            parts.append((at, jnp.dot(held[i], chosen, preferred_element_type=F32)))
        for at, part in parts:
            total[at] = total[at] + part

    for clear in clears:
        clear.wait()

    def store(i):
        place, local = tile[i] // size, tile[i] % size
        out = iter(outs)
        for begin, length, _ in spans:
            begin = begin - first
            for low, high in parts:
                to = next(out)
                here = (local >= begin) & (local < begin + length) & (place >= low) & (place < high)

                @pl.when(here)
                def _(to=to, low=low, begin=begin, length=length):
                    at = (place - low) * length + local - begin
                    pltpu.make_async_copy(staged.at[i], to.at[at], tile_sems.at[i]).start()

    @pl.loop(0, found)
    def _(i):
        staged[i] = total[i].astype(BF16)
        store(i)

    @pl.loop(0, found)
    def _(i):
        pltpu.make_async_copy(staged.at[i], outs[0].at[0], tile_sems.at[i]).wait()


def dense_sums(spans, peers, table, source, basis_in, basis_out, blocks):
    near_pairs, width, _ = blocks.shape
    far_pairs, rank, _ = basis_in.shape
    depth = source.shape[2]
    size = sum(length for _, length, _ in spans)
    most = min(peers * size, near_pairs + far_pairs)
    shapes, clears, span = [], 0, 16
    for _, length, _ in spans:
        for low, high in ranges(peers):
            tiles = (high - low) * length
            shapes.append(jax.ShapeDtypeStruct((tiles, width, depth), BF16))
            clears += -(-tiles // span)
    anywhere = pl.BlockSpec(memory_space=pl.ANY)
    outs = pl.pallas_call(
        functools.partial(sums_kernel, spans, peers, near_pairs, far_pairs),
        out_shape=tuple(shapes),
        in_specs=[smem()] + [pl.BlockSpec(memory_space=pltpu.HBM)] * 4,
        out_specs=(anywhere,) * len(shapes),
        scratch_shapes=[
            pltpu.VMEM((most + 1, width, depth), F32),
            pltpu.VMEM((near_pairs + GROUP, width, width), BF16),
            pltpu.VMEM((far_pairs + GROUP, 2 * rank, depth), BF16),
            pltpu.VMEM((span, width, depth), BF16),
            pltpu.VMEM((most, width, depth), BF16),
            pltpu.VMEM(source.shape, BF16),
            pltpu.VMEM(basis_in.shape, BF16),
            pltpu.VMEM(basis_out.shape, BF16),
            pltpu.SMEM((near_pairs + GROUP + 1,), I32),
            pltpu.SMEM((far_pairs + GROUP + 1,), I32),
            pltpu.SMEM((peers * size,), I32),
            pltpu.SMEM((most,), I32),
            pltpu.SemaphoreType.DMA((3,)),
            pltpu.SemaphoreType.DMA((near_pairs,)),
            pltpu.SemaphoreType.DMA((clears,)),
            pltpu.SemaphoreType.DMA((most,)),
        ],
        compiler_params=pltpu.CompilerParams(vmem_limit_bytes=VMEM_BYTES),
        cost_estimate=NO_COST,
        name="dense_sums",
    )(table, source, basis_in, basis_out, blocks)
    got = []
    for j, (_, length, _) in enumerate(spans):
        tile = (length, width, depth)
        leads = ((peers // 4,), (peers // 4,), (peers // 2,))
        got.append([out.reshape(lead + tile) for out, lead in zip(outs[3 * j : 3 * j + 3], leads)])
    return got


def pack_kernel(volume, stiffness, out):
    planes, cy, cz = volume.shape
    lanes = iota((cy, cz), 1)
    packed = jnp.zeros((cy, cz), F32)
    rows = iota((cy, cz), 0)

    def place(packed, column, at):
        return jnp.where(lanes == at, column, packed)

    for x in range(planes):
        here = volume[x]
        beside = jnp.where(rows == 0, 0.0, pltpu.roll(here, 1, 0))
        beside = beside + jnp.where(rows == cy - 1, 0.0, pltpu.roll(here, cy - 1, 0))
        if x > 0:
            beside = beside + volume[x - 1]
        if x < planes - 1:
            beside = beside + volume[x + 1]
        face = (6.0 + stiffness[x]) * here - beside
        column = face[:, 0:1] - here[:, 1:2]
        packed = place(packed, column, x)
    packed = place(packed, volume[0][:, 0:1], planes)
    packed = place(packed, volume[planes - 1][:, 0:1], planes + 1)
    packed = packed.T[: out.shape[1]]
    for n in range(out.shape[0]):
        out[n] = packed


def pack_face(peers, volume, stiffness):
    planes, cy, cz = volume.shape
    return pl.pallas_call(
        pack_kernel,
        out_shape=jax.ShapeDtypeStruct((peers, -(-(planes + 2) // 8) * 8, cy), F32),
        in_specs=[vmem()] * 2,
        out_specs=vmem(),
        compiler_params=pltpu.CompilerParams(vmem_limit_bytes=VMEM_BYTES),
        cost_estimate=NO_COST,
        name="pack_face",
    )(volume, stiffness)


def stencil_kernel(volume, stiffness, before, after, out):
    planes, cy, cz = volume.shape
    rows = iota((cy, cz), 0)
    lanes = iota((cy, cz), 1)
    for x in range(planes):
        here = volume[x]
        beside = (volume[x + 1] if x < planes - 1 else after[0]) + (volume[x - 1] if x > 0 else before[0])
        beside = beside + jnp.where(rows == cy - 1, 0.0, pltpu.roll(here, cy - 1, 0))
        beside = beside + jnp.where(rows == 0, 0.0, pltpu.roll(here, 1, 0))
        beside = beside + jnp.where(lanes == cz - 1, 0.0, pltpu.roll(here, cz - 1, 1))
        beside = beside + jnp.where(lanes == 0, 0.0, pltpu.roll(here, 1, 1))
        out[x] = (6.0 + stiffness[x]) * here - beside


def stencil(volume, stiffness, before, after):
    return pl.pallas_call(
        stencil_kernel,
        out_shape=jax.ShapeDtypeStruct(volume.shape, F32),
        in_specs=[vmem()] * 4,
        out_specs=vmem(),
        compiler_params=pltpu.CompilerParams(vmem_limit_bytes=VMEM_BYTES),
        cost_estimate=NO_COST,
        name="stencil",
    )(volume, stiffness, before, after)


def trace_kernel(
    ns, target, count, packs, places, far_blocks, basis_in, basis_out, far_source, far_target,
    traces, images, face, near_blocks, sem,
):
    load = pltpu.make_async_copy(far_blocks, near_blocks, sem)
    load.start()
    peers, _, cy = packs.shape
    nx = face.shape[0]
    planes = nx // peers
    clusters, width = places.shape
    rows8 = iota((planes, cy), 0)
    for n in range(peers):
        part = packs[n, 0:planes, :]
        if n > 0:
            part = part - jnp.where(rows8 == 0, packs[n - 1, planes + 1 : planes + 2, :], 0.0)
        if n < peers - 1:
            part = part - jnp.where(rows8 == planes - 1, packs[n + 1, planes : planes + 1, :], 0.0)
        face[n * planes : (n + 1) * planes, :] = part
    turned = jnp.concatenate(pieces(face[...].T, 3), axis=0)
    x_rows = iota((nx, width), 0)
    y_rows = iota((cy, width), 0)
    shift = cy.bit_length() - 1

    @pl.loop(0, clusters, unroll=4)
    def _(c):
        place = places[pl.ds(c, 1), :]
        picks = jnp.where(x_rows == (place >> shift), 1.0, 0.0).astype(BF16)
        columns = jnp.dot(turned, picks, preferred_element_type=F32)
        columns = columns[:cy] + columns[cy : 2 * cy] + columns[2 * cy :]
        found = jnp.where(y_rows == (place & (cy - 1)), columns, 0.0)
        traces[pl.ds(c, 1), :] = jnp.sum(found, axis=0, keepdims=True)

    contract = (((1,), (1,)), ((), ()))
    stacked = jnp.concatenate(pieces(traces[...], 2), axis=0)
    coefficients = lax.dot_general(stacked, basis_in[...], contract, preferred_element_type=F32)
    coefficients = coefficients[:clusters] + coefficients[clusters:]
    pairs_k = coefficients.shape[1]
    coefficients = jnp.where(iota((clusters, pairs_k), 0) == far_source[...], coefficients, 0.0)
    coefficients = jnp.sum(coefficients, axis=0, keepdims=True)
    block = 128

    @pl.loop(0, images.shape[0] // block)
    def _(b):
        base = pl.multiple_of(b * block, block)
        spread = jnp.where(iota((block, pairs_k), 0) + base == far_target[...], coefficients, 0.0)
        image = jnp.zeros((block, width), F32)
        for part in pieces(spread, 2):
            image = image + jnp.dot(part, basis_out[...], preferred_element_type=F32)
        images[pl.ds(base, block), :] = image

    lanes = iota((8, width), 1)
    rows = iota((8, width), 0)
    load.wait()
    group = math.gcd(near_blocks.shape[0], GROUP)

    @pl.loop(0, near_blocks.shape[0] // group)
    def _(g):
        parts = []
        for u in range(group):
            p = g * group + u
            at = target[p]
            trace = traces[pl.ds(ns[p], 1), :]
            placed = jnp.where((rows == (at & 7)) & (lanes < count[p]), trace, 0.0)
            both = jnp.concatenate(pieces(placed, 2), axis=0)
            image = lax.dot_general(both, near_blocks[p], contract, preferred_element_type=F32)
            parts.append((pl.multiple_of((at >> 3) * 8, 8), image[:8] + image[8:]))
        for base, image in parts:
            images[pl.ds(base, 8), :] = images[pl.ds(base, 8), :] + image


def trace_images(peers, nx, ns, target, count, packs, places, near_blocks, basis_in, basis_out, far_source, far_target):
    clusters, width = places.shape
    pairs, rank, _ = basis_in.shape
    return pl.pallas_call(
        trace_kernel,
        out_shape=(
            jax.ShapeDtypeStruct((clusters, width), F32),
            jax.ShapeDtypeStruct((peers * clusters, width), F32),
        ),
        in_specs=[smem()] * 3 + [vmem()] * 2 + [pl.BlockSpec(memory_space=pl.ANY)] + [vmem()] * 4,
        out_specs=(vmem(), vmem()),
        scratch_shapes=[
            pltpu.VMEM((nx, packs.shape[2]), F32),
            pltpu.VMEM(near_blocks.shape, BF16),
            pltpu.SemaphoreType.DMA(()),
        ],
        compiler_params=pltpu.CompilerParams(vmem_limit_bytes=VMEM_BYTES),
        cost_estimate=NO_COST,
        name="trace_images",
    )(
        ns, target, count, packs, places, near_blocks,
        basis_in.reshape(pairs * rank, width), basis_out.reshape(pairs * rank, width),
        jnp.repeat(far_source, rank)[None, :], jnp.repeat(far_target, rank)[None, :],
    )


def sum_kernel(groups, *refs):
    outs = refs[len(refs) - len(groups) :]
    for out, group in zip(outs, groups):
        total = None
        for operand, index in group:
            term = refs[operand][index].astype(F32)
            total = term if total is None else total + term
        out[...] = total.astype(out.dtype)


def tile_sums(grid, groups, operands, outputs, aliases={}):
    return pl.pallas_call(
        functools.partial(sum_kernel, groups),
        grid=(grid,),
        out_shape=tuple(shape for shape, _, _ in outputs),
        in_specs=[pl.BlockSpec(block, index) for _, block, index in operands],
        out_specs=tuple(pl.BlockSpec(block, index) for _, block, index in outputs),
        input_output_aliases=aliases,
        compiler_params=pltpu.CompilerParams(vmem_limit_bytes=VMEM_BYTES),
        cost_estimate=NO_COST,
        name="tile_sums",
    )(*[array for array, _, _ in operands])


def block_of(size, most):
    return max(d for d in range(1, max(1, min(size, most)) + 1) if size % d == 0)


def half_sum(keep, other):
    places, tile = other.shape[0], other.shape[1:]
    step = max(1, places // 2)
    zeros = (0,) * len(tile)
    block = (step,) + tile
    return tile_sums(
        places // step, [[(0, ...), (1, ...)]],
        [(keep, block, lambda i: (places // step + i,) + zeros), (other, block, lambda i: (i,) + zeros)],
        [(jax.ShapeDtypeStruct(other.shape, BF16), block, lambda i: (i,) + zeros)],
    )[0]


def later_sum(places, *terms):
    size, width, depth = terms[0].shape[1:]
    step = block_of(size, 10 // places)
    block = (places, step, width, depth)
    return tile_sums(
        size // step, [[(i, ...) for i in range(len(terms))]],
        [(term, block, lambda i: (1, i, 0, 0)) for term in terms],
        [(jax.ShapeDtypeStruct((places, size, width, depth), BF16), block, lambda i: (0, i, 0, 0))],
    )[0]


def result(first, out, *terms):
    size, width, depth = terms[0].shape[1:]
    step = block_of(size, 5)
    while first % step:
        step = block_of(size, step - 1)
    tile = (step, width, depth)
    here = (out, tile, lambda i: (first // step + i, 0, 0))
    operands = [here] + [(term, (None,) + tile, lambda i: (0, i, 0, 0)) for term in terms]
    return tile_sums(
        size // step, [[(i, ...) for i in range(len(operands))]], operands,
        [(jax.ShapeDtypeStruct(out.shape, F32),) + here[1:]], {0: 0},
    )[0]


def swap(value, bit):
    peers = lax.axis_size("clus")
    return lax.ppermute(value, "clus", [(i, i ^ bit) for i in range(peers)])


class Sent:
    def __init__(self, value):
        self.value = value


class Order:
    def __init__(self, token):
        self.token = token
        self.sent, self.later, self.late = [], [], False

    def send(self, value):
        sent = Sent(value)
        (self.later if self.late else self.sent).append(sent)
        return sent

    def wait(self):
        values = self(lambda *a: a, *[sent.value for sent in self.sent])
        for sent, value in zip(self.sent, values):
            sent.value = value
        self.sent, self.later = self.later, []

    def __call__(self, act, *args):
        args, _ = lax.optimization_barrier((args, self.token))
        out = act(*args)
        self.token = jax.tree.leaves(out)[0]
        return out


def body(
    adjoint_volume,
    stiffness,
    boundary_source,
    trace_gain,
    trace_map,
    near_blocks,
    near_source,
    near_target_dev,
    near_target_local,
    close_block_column_count,
    far_basis_in,
    far_basis_out,
    far_source,
    far_target_dev,
    far_target_local,
):
    peers = lax.axis_size("clus")
    clusters = boundary_source.shape[0]
    planes = adjoint_volume.shape[0]
    near_owner = near_target_dev.reshape(-1)
    far_owner = far_target_dev.reshape(-1)
    table = jnp.concatenate([
        near_source, near_owner, near_target_local, close_block_column_count,
        far_source, far_owner, far_target_local,
    ])
    near_target = near_owner * clusters + near_target_local
    far_target = far_owner * clusters + far_target_local
    order = Order(table)
    got = {}

    def sums():
        for call in range(1 + max(call for _, _, call in PLAN)):
            chunks = [j for j, plan in enumerate(PLAN) if plan[2] == call]
            pairs = order(
                lambda *a: dense_sums([spans[j] for j in chunks], peers, *a),
                table, boundary_source, far_basis_in, far_basis_out, near_blocks,
            )
            for j, pair in zip(chunks, pairs):
                got[j] = pair
            yield

    def chunk(j):
        same, other, keep = got[j]
        bits = order_of(peers, PLAN[j][1])[1:]
        other, same = order.send(swap(other, 1)), order.send(swap(same, 1))
        yield
        sent = [order.send(swap(order(half_sum, keep, other.value), bits[0]))]
        yield
        places = peers // 8
        for step, bit in enumerate(bits[1:]):
            terms = [keep, same.value] + [each.value for each in sent]
            sent.append(order.send(swap(order(functools.partial(later_sum, places), *terms), bit)))
            if step == 0 or places == 1:
                yield
            places //= 2
        terms = [keep, same.value] + [each.value for each in sent]
        got["out"] = order(functools.partial(result, spans[j][0]), got["out"], *terms)
        yield

    def exchange(value):
        return order.send(lax.all_to_all(value, "clus", split_axis=0, concat_axis=0, tiled=True))

    def face():
        packs = exchange(order(functools.partial(pack_face, peers), adjoint_volume, stiffness))
        yield
        traces, images = order(
            lambda packs, near: trace_images(
                peers, planes * peers, near_source, near_target, close_block_column_count,
                packs, trace_map, near, far_basis_in, far_basis_out, far_source, far_target,
            ),
            packs.value, near_blocks,
        )
        images = exchange(images.reshape((peers, clusters) + images.shape[1:]))
        yield
        got["out"] = order(
            lambda out, g, t, i: out + (t + jnp.sum(i, axis=0))[:, :, None] * g[None, None, :],
            got["out"], trace_gain, traces, images.value,
        )
        yield

    def base():
        got["out"] = order(lambda s: s.astype(F32), boundary_source)
        yield

    def volume():
        ends = peers - 1
        tail, head = order(lambda v: (v[planes - 1 :], v[:1]), adjoint_volume)
        before = order.send(lax.ppermute(tail, "clus", [(i, i + 1) for i in range(ends)]))
        after = order.send(lax.ppermute(head, "clus", [(i + 1, i) for i in range(ends)]))
        yield
        got["volume"] = order(stencil, adjoint_volume, stiffness, before.value, after.value)
        yield

    spans, first = [], 0
    for share, z_first, _ in PLAN:
        spans.append((first, share * clusters // 16, z_first))
        first += spans[-1][1]
    runs = {"s": sums(), "f": face(), "v": volume(), "b": base()}
    runs.update((str(j), chunk(j)) for j in range(len(PLAN)))
    for name in SEQUENCE:
        if name == "w":
            order.wait()
        elif name != "l":
            next(runs[name])
        order.late = name == "l"
    return got["volume"], got["out"]


def solution(mesh):
    whole = ("groups", "clus")
    one, two, three = P(whole), P(whole, None), P(whole, None, None)
    return jax.shard_map(
        body,
        mesh=mesh,
        in_specs=(three, three, three, P(), two, three, one, two, one, one, three, three, one, two, one),
        out_specs=(three, three),
        check_vma=False,
    )
```

```python
import functools
import math

import jax
import jax.numpy as jnp
from jax import lax
from jax.experimental import pallas as pl
from jax.experimental.pallas import tpu as pltpu
from jax.sharding import PartitionSpec as P

F32 = jnp.float32
BF16 = jnp.bfloat16
I32 = jnp.int32
MIB = 1 << 20
VMEM_BYTES = 60 * MIB
NO_COST = pl.CostEstimate(flops=1, bytes_accessed=1, transcendentals=0)

PLAN = ((5, False, 0), (5, True, 0), (4, False, 1), (2, False, 1))

SEQUENCE = tuple("s0101s23lfbw20l1w203lflvw1320vw3f12w3")


def smem():
    return pl.BlockSpec(memory_space=pltpu.SMEM)


def vmem():
    return pl.BlockSpec(memory_space=pltpu.VMEM)


def iota(shape, dim):
    return lax.broadcasted_iota(I32, shape, dim)


def pieces(value, count):
    out = []
    for _ in range(count):
        part = value.astype(BF16)
        out.append(part)
        value = value - part.astype(F32)
    return out


GROUP = 16


def order_of(peers, z_first):
    z = []
    bit = 4
    while bit < peers:
        z.append(bit)
        bit *= 2
    return [1] + z + [2] if z_first else [1, 2] + z


def place_of(apart, bits):
    place = 0
    for bit in bits:
        place = place * 2 + jnp.where((apart & bit) != 0, 1, 0)
    return place


def ranges(peers):
    return ((peers // 2, 3 * peers // 4), (3 * peers // 4, peers), (0, peers // 2))


def sums_kernel(spans, peers, near_pairs, far_pairs, table, far_source, far_in, far_out, blocks, *refs):
    parts = ranges(peers)
    outs = refs[: len(spans) * len(parts)]
    (total, held, coefficients, zeros, staged, source, basis_in, basis_out, near_list, far_list, rank, tile,
     load_sems, block_sems, zero_sems, tile_sems) = refs[len(outs) :]
    loads = [
        pltpu.make_async_copy(whole, part, load_sems.at[i])
        for i, (whole, part) in enumerate(((far_source, source), (far_in, basis_in), (far_out, basis_out)))
    ]
    for load in loads:
        load.start()
    me = lax.axis_index("clus")
    half = peers // 2
    first = spans[0][0]
    size = sum(length for _, length, _ in spans)
    tiles = peers * size
    ns, nd, nl, count, fs, fd, fl = [
        (lambda at: lambda p: table[at + p])(at)
        for at in (0, near_pairs, 2 * near_pairs, 3 * near_pairs, 4 * near_pairs, 4 * near_pairs + far_pairs, 4 * near_pairs + 2 * far_pairs)
    ]
    spare = total.shape[0] - 1

    def compact(local, listing, pairs):
        def step(p, found):
            at = local(p)
            listing[found] = p
            return found + jnp.where((at >= first) & (at < first + size), 1, 0)

        found = lax.fori_loop(0, pairs, step, 0, unroll=8)
        for u in range(GROUP):
            listing[found + u] = 0
        return found

    zeros[...] = jnp.zeros(zeros.shape, BF16)
    span = zeros.shape[0]
    clears = []
    for out in outs:
        for at in range(0, out.shape[0], span):
            here = min(span, out.shape[0] - at)
            clears.append(
                pltpu.make_async_copy(zeros.at[pl.ds(0, here)], out.at[pl.ds(at, here)], zero_sems.at[len(clears)])
            )

    nears = compact(nl, near_list, near_pairs)

    def fetch(i):
        return pltpu.make_async_copy(blocks.at[near_list[i]], held.at[i], block_sems.at[i])

    @pl.loop(0, nears)
    def _(i):
        fetch(i).start()

    for clear in clears:
        clear.start()
    fars = compact(fl, far_list, far_pairs)

    @pl.loop(0, tiles // 8)
    def _(i):
        for u in range(8):
            rank[i * 8 + u] = -1

    def slot(device, local):
        place = place_of(device ^ me, order_of(peers, spans[0][2]))
        for begin, length, z_first in spans[1:]:
            if z_first != spans[0][2]:
                here = (local >= begin) & (local < begin + length)
                place = jnp.where(here, place_of(device ^ me, order_of(peers, z_first)), place)
        return place * size + local - first

    def visit(at, found):
        fresh = rank[at] < 0

        @pl.when(fresh)
        def _():
            rank[at] = found
            tile[found] = at
            total[found] = jnp.zeros(total.shape[1:], F32)

        return found + jnp.where(fresh, 1, 0)

    def visit_far(i, found):
        p = far_list[i]
        return visit(slot(fd(p), fl(p)), found)

    def visit_near(i, found):
        p = near_list[i]
        return visit(slot(nd(p), nl(p)), found)

    found = lax.fori_loop(0, fars, visit_far, 0)
    found = lax.fori_loop(0, nears, visit_near, found)

    for load in loads:
        load.wait()

    @pl.loop(0, (fars + GROUP - 1) // GROUP)
    def _(g):
        for u in range(GROUP):
            p = far_list[g * GROUP + u]
            value = jnp.dot(basis_in[p], source[fs(p)], preferred_element_type=F32)
            coefficients[g * GROUP + u] = jnp.concatenate(pieces(value, 2), axis=0)

    @pl.loop(0, (fars + GROUP - 1) // GROUP)
    def _(g):
        parts = []
        for u in range(GROUP):
            i = g * GROUP + u
            p = far_list[i]
            basis = jnp.concatenate([basis_out[p], basis_out[p]], axis=0)
            at = jnp.where(i < fars, rank[slot(fd(p), jnp.where(i < fars, fl(p), first))], spare)
            parts.append((at, lax.dot_general(basis, coefficients[i], (((0,), (0,)), ((), ())), preferred_element_type=F32)))
        for at, part in parts:
            total[at] = total[at] + part

    rows = iota(source.shape[1:], 0)

    @pl.loop(0, (nears + GROUP - 1) // GROUP)
    def _(g):
        parts = []
        for u in range(GROUP):
            i = g * GROUP + u

            @pl.when(i < nears)
            def _():
                fetch(i).wait()

        for u in range(GROUP):
            i = g * GROUP + u
            p = near_list[i]
            chosen = jnp.where(rows < count(p), source[ns(p)].astype(F32), 0.0).astype(BF16)
            at = jnp.where(i < nears, rank[slot(nd(p), jnp.where(i < nears, nl(p), first))], spare)
            parts.append((at, jnp.dot(held[i], chosen, preferred_element_type=F32)))
        for at, part in parts:
            total[at] = total[at] + part

    for clear in clears:
        clear.wait()

    def store(i):
        place, local = tile[i] // size, tile[i] % size
        out = iter(outs)
        for begin, length, _ in spans:
            begin = begin - first
            for low, high in parts:
                to = next(out)
                here = (local >= begin) & (local < begin + length) & (place >= low) & (place < high)

                @pl.when(here)
                def _(to=to, low=low, begin=begin, length=length):
                    at = (place - low) * length + local - begin
                    pltpu.make_async_copy(staged.at[i], to.at[at], tile_sems.at[i]).start()

    @pl.loop(0, found)
    def _(i):
        staged[i] = total[i].astype(BF16)
        store(i)

    @pl.loop(0, found)
    def _(i):
        pltpu.make_async_copy(staged.at[i], outs[0].at[0], tile_sems.at[i]).wait()


def dense_sums(spans, peers, table, source, basis_in, basis_out, blocks):
    near_pairs, width, _ = blocks.shape
    far_pairs, rank, _ = basis_in.shape
    depth = source.shape[2]
    size = sum(length for _, length, _ in spans)
    most = min(peers * size, near_pairs + far_pairs)
    shapes, clears, span = [], 0, 16
    for _, length, _ in spans:
        for low, high in ranges(peers):
            tiles = (high - low) * length
            shapes.append(jax.ShapeDtypeStruct((tiles, width, depth), BF16))
            clears += -(-tiles // span)
    anywhere = pl.BlockSpec(memory_space=pl.ANY)
    outs = pl.pallas_call(
        functools.partial(sums_kernel, spans, peers, near_pairs, far_pairs),
        out_shape=tuple(shapes),
        in_specs=[smem()] + [pl.BlockSpec(memory_space=pltpu.HBM)] * 4,
        out_specs=(anywhere,) * len(shapes),
        scratch_shapes=[
            pltpu.VMEM((most + 1, width, depth), F32),
            pltpu.VMEM((near_pairs + GROUP, width, width), BF16),
            pltpu.VMEM((far_pairs + GROUP, 2 * rank, depth), BF16),
            pltpu.VMEM((span, width, depth), BF16),
            pltpu.VMEM((most, width, depth), BF16),
            pltpu.VMEM(source.shape, BF16),
            pltpu.VMEM(basis_in.shape, BF16),
            pltpu.VMEM(basis_out.shape, BF16),
            pltpu.SMEM((near_pairs + GROUP + 1,), I32),
            pltpu.SMEM((far_pairs + GROUP + 1,), I32),
            pltpu.SMEM((peers * size,), I32),
            pltpu.SMEM((most,), I32),
            pltpu.SemaphoreType.DMA((3,)),
            pltpu.SemaphoreType.DMA((near_pairs,)),
            pltpu.SemaphoreType.DMA((clears,)),
            pltpu.SemaphoreType.DMA((most,)),
        ],
        compiler_params=pltpu.CompilerParams(vmem_limit_bytes=VMEM_BYTES),
        cost_estimate=NO_COST,
        name="dense_sums",
    )(table, source, basis_in, basis_out, blocks)
    got = []
    for j, (_, length, _) in enumerate(spans):
        tile = (length, width, depth)
        leads = ((peers // 4,), (peers // 4,), (peers // 2,))
        got.append([out.reshape(lead + tile) for out, lead in zip(outs[3 * j : 3 * j + 3], leads)])
    return got


def pack_kernel(volume, stiffness, out):
    planes, cy, cz = volume.shape
    lanes = iota((cy, cz), 1)
    packed = jnp.zeros((cy, cz), F32)
    rows = iota((cy, cz), 0)

    def place(packed, column, at):
        return jnp.where(lanes == at, column, packed)

    for x in range(planes):
        here = volume[x]
        beside = jnp.where(rows == 0, 0.0, pltpu.roll(here, 1, 0))
        beside = beside + jnp.where(rows == cy - 1, 0.0, pltpu.roll(here, cy - 1, 0))
        if x > 0:
            beside = beside + volume[x - 1]
        if x < planes - 1:
            beside = beside + volume[x + 1]
        face = (6.0 + stiffness[x]) * here - beside
        column = face[:, 0:1] - here[:, 1:2]
        packed = place(packed, column, x)
    packed = place(packed, volume[0][:, 0:1], planes)
    packed = place(packed, volume[planes - 1][:, 0:1], planes + 1)
    packed = packed.T[: out.shape[1]]
    for n in range(out.shape[0]):
        out[n] = packed


def pack_face(peers, volume, stiffness):
    planes, cy, cz = volume.shape
    return pl.pallas_call(
        pack_kernel,
        out_shape=jax.ShapeDtypeStruct((peers, -(-(planes + 2) // 8) * 8, cy), F32),
        in_specs=[vmem()] * 2,
        out_specs=vmem(),
        compiler_params=pltpu.CompilerParams(vmem_limit_bytes=VMEM_BYTES),
        cost_estimate=NO_COST,
        name="pack_face",
    )(volume, stiffness)


def stencil_kernel(volume, stiffness, before, after, out):
    planes, cy, cz = volume.shape
    rows = iota((cy, cz), 0)
    lanes = iota((cy, cz), 1)
    for x in range(planes):
        here = volume[x]
        beside = (volume[x + 1] if x < planes - 1 else after[0]) + (volume[x - 1] if x > 0 else before[0])
        beside = beside + jnp.where(rows == cy - 1, 0.0, pltpu.roll(here, cy - 1, 0))
        beside = beside + jnp.where(rows == 0, 0.0, pltpu.roll(here, 1, 0))
        beside = beside + jnp.where(lanes == cz - 1, 0.0, pltpu.roll(here, cz - 1, 1))
        beside = beside + jnp.where(lanes == 0, 0.0, pltpu.roll(here, 1, 1))
        out[x] = (6.0 + stiffness[x]) * here - beside


def stencil(volume, stiffness, before, after):
    return pl.pallas_call(
        stencil_kernel,
        out_shape=jax.ShapeDtypeStruct(volume.shape, F32),
        in_specs=[vmem()] * 4,
        out_specs=vmem(),
        compiler_params=pltpu.CompilerParams(vmem_limit_bytes=VMEM_BYTES),
        cost_estimate=NO_COST,
        name="stencil",
    )(volume, stiffness, before, after)


def trace_kernel(
    ns, target, count, packs, places, far_blocks, basis_in, basis_out, far_source, far_target,
    traces, images, face, near_blocks, sem,
):
    load = pltpu.make_async_copy(far_blocks, near_blocks, sem)
    load.start()
    peers, _, cy = packs.shape
    nx = face.shape[0]
    planes = nx // peers
    clusters, width = places.shape
    rows8 = iota((planes, cy), 0)
    for n in range(peers):
        part = packs[n, 0:planes, :]
        if n > 0:
            part = part - jnp.where(rows8 == 0, packs[n - 1, planes + 1 : planes + 2, :], 0.0)
        if n < peers - 1:
            part = part - jnp.where(rows8 == planes - 1, packs[n + 1, planes : planes + 1, :], 0.0)
        face[n * planes : (n + 1) * planes, :] = part
    turned = jnp.concatenate(pieces(face[...].T, 3), axis=0)
    x_rows = iota((nx, width), 0)
    y_rows = iota((cy, width), 0)
    shift = cy.bit_length() - 1

    @pl.loop(0, clusters, unroll=4)
    def _(c):
        place = places[pl.ds(c, 1), :]
        picks = jnp.where(x_rows == (place >> shift), 1.0, 0.0).astype(BF16)
        columns = jnp.dot(turned, picks, preferred_element_type=F32)
        columns = columns[:cy] + columns[cy : 2 * cy] + columns[2 * cy :]
        found = jnp.where(y_rows == (place & (cy - 1)), columns, 0.0)
        traces[pl.ds(c, 1), :] = jnp.sum(found, axis=0, keepdims=True)

    contract = (((1,), (1,)), ((), ()))
    stacked = jnp.concatenate(pieces(traces[...], 2), axis=0)
    coefficients = lax.dot_general(stacked, basis_in[...], contract, preferred_element_type=F32)
    coefficients = coefficients[:clusters] + coefficients[clusters:]
    pairs_k = coefficients.shape[1]
    coefficients = jnp.where(iota((clusters, pairs_k), 0) == far_source[...], coefficients, 0.0)
    coefficients = jnp.sum(coefficients, axis=0, keepdims=True)
    block = 128

    @pl.loop(0, images.shape[0] // block)
    def _(b):
        base = pl.multiple_of(b * block, block)
        spread = jnp.where(iota((block, pairs_k), 0) + base == far_target[...], coefficients, 0.0)
        image = jnp.zeros((block, width), F32)
        for part in pieces(spread, 2):
            image = image + jnp.dot(part, basis_out[...], preferred_element_type=F32)
        images[pl.ds(base, block), :] = image

    lanes = iota((8, width), 1)
    rows = iota((8, width), 0)
    load.wait()
    group = math.gcd(near_blocks.shape[0], GROUP)

    @pl.loop(0, near_blocks.shape[0] // group)
    def _(g):
        parts = []
        for u in range(group):
            p = g * group + u
            at = target[p]
            trace = traces[pl.ds(ns[p], 1), :]
            placed = jnp.where((rows == (at & 7)) & (lanes < count[p]), trace, 0.0)
            both = jnp.concatenate(pieces(placed, 2), axis=0)
            image = lax.dot_general(both, near_blocks[p], contract, preferred_element_type=F32)
            parts.append((pl.multiple_of((at >> 3) * 8, 8), image[:8] + image[8:]))
        for base, image in parts:
            images[pl.ds(base, 8), :] = images[pl.ds(base, 8), :] + image


def trace_images(peers, nx, ns, target, count, packs, places, near_blocks, basis_in, basis_out, far_source, far_target):
    clusters, width = places.shape
    pairs, rank, _ = basis_in.shape
    return pl.pallas_call(
        trace_kernel,
        out_shape=(
            jax.ShapeDtypeStruct((clusters, width), F32),
            jax.ShapeDtypeStruct((peers * clusters, width), F32),
        ),
        in_specs=[smem()] * 3 + [vmem()] * 2 + [pl.BlockSpec(memory_space=pl.ANY)] + [vmem()] * 4,
        out_specs=(vmem(), vmem()),
        scratch_shapes=[
            pltpu.VMEM((nx, packs.shape[2]), F32),
            pltpu.VMEM(near_blocks.shape, BF16),
            pltpu.SemaphoreType.DMA(()),
        ],
        compiler_params=pltpu.CompilerParams(vmem_limit_bytes=VMEM_BYTES),
        cost_estimate=NO_COST,
        name="trace_images",
    )(
        ns, target, count, packs, places, near_blocks,
        basis_in.reshape(pairs * rank, width), basis_out.reshape(pairs * rank, width),
        jnp.repeat(far_source, rank)[None, :], jnp.repeat(far_target, rank)[None, :],
    )


def sum_kernel(groups, *refs):
    outs = refs[len(refs) - len(groups) :]
    for out, group in zip(outs, groups):
        total = None
        for operand, index in group:
            term = refs[operand][index].astype(F32)
            total = term if total is None else total + term
        out[...] = total.astype(out.dtype)


def tile_sums(grid, groups, operands, outputs, aliases={}):
    return pl.pallas_call(
        functools.partial(sum_kernel, groups),
        grid=(grid,),
        out_shape=tuple(shape for shape, _, _ in outputs),
        in_specs=[pl.BlockSpec(block, index) for _, block, index in operands],
        out_specs=tuple(pl.BlockSpec(block, index) for _, block, index in outputs),
        input_output_aliases=aliases,
        compiler_params=pltpu.CompilerParams(vmem_limit_bytes=VMEM_BYTES),
        cost_estimate=NO_COST,
        name="tile_sums",
    )(*[array for array, _, _ in operands])


def block_of(size, most):
    return max(d for d in range(1, max(1, min(size, most)) + 1) if size % d == 0)


def half_sum(keep, other):
    places, tile = other.shape[0], other.shape[1:]
    step = max(1, places // 2)
    zeros = (0,) * len(tile)
    block = (step,) + tile
    return tile_sums(
        places // step, [[(0, ...), (1, ...)]],
        [(keep, block, lambda i: (places // step + i,) + zeros), (other, block, lambda i: (i,) + zeros)],
        [(jax.ShapeDtypeStruct(other.shape, BF16), block, lambda i: (i,) + zeros)],
    )[0]


def later_sum(places, *terms):
    size, width, depth = terms[0].shape[1:]
    step = block_of(size, 10 // places)
    block = (places, step, width, depth)
    return tile_sums(
        size // step, [[(i, ...) for i in range(len(terms))]],
        [(term, block, lambda i: (1, i, 0, 0)) for term in terms],
        [(jax.ShapeDtypeStruct((places, size, width, depth), BF16), block, lambda i: (0, i, 0, 0))],
    )[0]


def result(first, out, *terms):
    size, width, depth = terms[0].shape[1:]
    step = block_of(size, 5)
    while first % step:
        step = block_of(size, step - 1)
    tile = (step, width, depth)
    here = (out, tile, lambda i: (first // step + i, 0, 0))
    operands = [here] + [(term, (None,) + tile, lambda i: (0, i, 0, 0)) for term in terms]
    return tile_sums(
        size // step, [[(i, ...) for i in range(len(operands))]], operands,
        [(jax.ShapeDtypeStruct(out.shape, F32),) + here[1:]], {0: 0},
    )[0]


def swap(value, bit):
    peers = lax.axis_size("clus")
    return lax.ppermute(value, "clus", [(i, i ^ bit) for i in range(peers)])


class Sent:
    def __init__(self, value):
        self.value = value


class Order:
    def __init__(self, token):
        self.token = token
        self.sent, self.later, self.late = [], [], False

    def send(self, value):
        sent = Sent(value)
        (self.later if self.late else self.sent).append(sent)
        return sent

    def wait(self):
        values = self(lambda *a: a, *[sent.value for sent in self.sent])
        for sent, value in zip(self.sent, values):
            sent.value = value
        self.sent, self.later = self.later, []

    def __call__(self, act, *args):
        args, _ = lax.optimization_barrier((args, self.token))
        out = act(*args)
        self.token = jax.tree.leaves(out)[0]
        return out


def body(
    adjoint_volume,
    stiffness,
    boundary_source,
    trace_gain,
    trace_map,
    near_blocks,
    near_source,
    near_target_dev,
    near_target_local,
    close_block_column_count,
    far_basis_in,
    far_basis_out,
    far_source,
    far_target_dev,
    far_target_local,
):
    peers = lax.axis_size("clus")
    clusters = boundary_source.shape[0]
    planes = adjoint_volume.shape[0]
    near_owner = near_target_dev.reshape(-1)
    far_owner = far_target_dev.reshape(-1)
    table = jnp.concatenate([
        near_source, near_owner, near_target_local, close_block_column_count,
        far_source, far_owner, far_target_local,
    ])
    near_target = near_owner * clusters + near_target_local
    far_target = far_owner * clusters + far_target_local
    order = Order(table)
    got = {}

    def sums():
        for call in range(1 + max(call for _, _, call in PLAN)):
            chunks = [j for j, plan in enumerate(PLAN) if plan[2] == call]
            pairs = order(
                lambda *a: dense_sums([spans[j] for j in chunks], peers, *a),
                table, boundary_source, far_basis_in, far_basis_out, near_blocks,
            )
            for j, pair in zip(chunks, pairs):
                got[j] = pair
            yield

    def chunk(j):
        same, other, keep = got[j]
        bits = order_of(peers, PLAN[j][1])[1:]
        other, same = order.send(swap(other, 1)), order.send(swap(same, 1))
        yield
        sent = [order.send(swap(order(half_sum, keep, other.value), bits[0]))]
        yield
        places = peers // 8
        for step, bit in enumerate(bits[1:]):
            terms = [keep, same.value] + [each.value for each in sent]
            sent.append(order.send(swap(order(functools.partial(later_sum, places), *terms), bit)))
            if step == 0 or places == 1:
                yield
            places //= 2
        terms = [keep, same.value] + [each.value for each in sent]
        got["out"] = order(functools.partial(result, spans[j][0]), got["out"], *terms)
        yield

    def exchange(value):
        return order.send(lax.all_to_all(value, "clus", split_axis=0, concat_axis=0, tiled=True))

    def face():
        packs = exchange(order(functools.partial(pack_face, peers), adjoint_volume, stiffness))
        yield
        traces, images = order(
            lambda packs, near: trace_images(
                peers, planes * peers, near_source, near_target, close_block_column_count,
                packs, trace_map, near, far_basis_in, far_basis_out, far_source, far_target,
            ),
            packs.value, near_blocks,
        )
        images = exchange(images.reshape((peers, clusters) + images.shape[1:]))
        yield
        got["out"] = order(
            lambda out, g, t, i: out + (t + jnp.sum(i, axis=0))[:, :, None] * g[None, None, :],
            got["out"], trace_gain, traces, images.value,
        )
        yield

    def base():
        got["out"] = order(lambda s: s.astype(F32), boundary_source)
        yield

    def volume():
        ends = peers - 1
        tail, head = order(lambda v: (v[planes - 1 :], v[:1]), adjoint_volume)
        before = order.send(lax.ppermute(tail, "clus", [(i, i + 1) for i in range(ends)]))
        after = order.send(lax.ppermute(head, "clus", [(i + 1, i) for i in range(ends)]))
        yield
        got["volume"] = order(stencil, adjoint_volume, stiffness, before.value, after.value)
        yield

    spans, first = [], 0
    for share, z_first, _ in PLAN:
        spans.append((first, share * clusters // 16, z_first))
        first += spans[-1][1]
    runs = {"s": sums(), "f": face(), "v": volume(), "b": base()}
    runs.update((str(j), chunk(j)) for j in range(len(PLAN)))
    for name in SEQUENCE:
        if name == "w":
            order.wait()
        elif name != "l":
            next(runs[name])
        order.late = name == "l"
    return got["volume"], got["out"]


def solution(mesh):
    whole = ("groups", "clus")
    one, two, three = P(whole), P(whole, None), P(whole, None, None)
    return jax.shard_map(
        body,
        mesh=mesh,
        in_specs=(three, three, three, P(), two, three, one, two, one, one, three, three, one, two, one),
        out_specs=(three, three),
        check_vma=False,
    )
```

```python
import functools
import math

import jax
import jax.numpy as jnp
from jax import lax
from jax.experimental import pallas as pl
from jax.experimental.pallas import tpu as pltpu
from jax.sharding import PartitionSpec as P

F32 = jnp.float32
BF16 = jnp.bfloat16
I32 = jnp.int32
MIB = 1 << 20
VMEM_BYTES = 60 * MIB
NO_COST = pl.CostEstimate(flops=1, bytes_accessed=1, transcendentals=0)

PLAN = ((5, False, 0), (5, True, 0), (4, False, 1), (2, False, 1))

SEQUENCE = tuple("s0101s23lfbw20l1w203lflvw2310w3f12vw3")


def smem():
    return pl.BlockSpec(memory_space=pltpu.SMEM)


def vmem():
    return pl.BlockSpec(memory_space=pltpu.VMEM)


def iota(shape, dim):
    return lax.broadcasted_iota(I32, shape, dim)


def pieces(value, count):
    out = []
    for _ in range(count):
        part = value.astype(BF16)
        out.append(part)
        value = value - part.astype(F32)
    return out


GROUP = 16


def order_of(peers, z_first):
    z = []
    bit = 4
    while bit < peers:
        z.append(bit)
        bit *= 2
    return [1] + z + [2] if z_first else [1, 2] + z


def place_of(apart, bits):
    place = 0
    for bit in bits:
        place = place * 2 + jnp.where((apart & bit) != 0, 1, 0)
    return place


def ranges(peers):
    return ((peers // 2, 3 * peers // 4), (3 * peers // 4, peers), (0, peers // 2))


def sums_kernel(spans, peers, near_pairs, far_pairs, table, far_source, far_in, far_out, blocks, *refs):
    parts = ranges(peers)
    outs = refs[: len(spans) * len(parts)]
    (total, held, coefficients, zeros, staged, source, basis_in, basis_out, near_list, far_list, rank, tile,
     load_sems, block_sems, zero_sems, tile_sems) = refs[len(outs) :]
    loads = [
        pltpu.make_async_copy(whole, part, load_sems.at[i])
        for i, (whole, part) in enumerate(((far_source, source), (far_in, basis_in), (far_out, basis_out)))
    ]
    for load in loads:
        load.start()
    me = lax.axis_index("clus")
    half = peers // 2
    first = spans[0][0]
    size = sum(length for _, length, _ in spans)
    tiles = peers * size
    ns, nd, nl, count, fs, fd, fl = [
        (lambda at: lambda p: table[at + p])(at)
        for at in (0, near_pairs, 2 * near_pairs, 3 * near_pairs, 4 * near_pairs, 4 * near_pairs + far_pairs, 4 * near_pairs + 2 * far_pairs)
    ]
    spare = total.shape[0] - 1

    def compact(local, listing, pairs):
        def step(p, found):
            at = local(p)
            listing[found] = p
            return found + jnp.where((at >= first) & (at < first + size), 1, 0)

        found = lax.fori_loop(0, pairs, step, 0, unroll=8)
        for u in range(GROUP):
            listing[found + u] = 0
        return found

    zeros[...] = jnp.zeros(zeros.shape, BF16)
    span = zeros.shape[0]
    clears = []
    for out in outs:
        for at in range(0, out.shape[0], span):
            here = min(span, out.shape[0] - at)
            clears.append(
                pltpu.make_async_copy(zeros.at[pl.ds(0, here)], out.at[pl.ds(at, here)], zero_sems.at[len(clears)])
            )

    nears = compact(nl, near_list, near_pairs)

    def fetch(i):
        return pltpu.make_async_copy(blocks.at[near_list[i]], held.at[i], block_sems.at[i])

    @pl.loop(0, nears)
    def _(i):
        fetch(i).start()

    for clear in clears:
        clear.start()
    fars = compact(fl, far_list, far_pairs)

    @pl.loop(0, tiles // 8)
    def _(i):
        for u in range(8):
            rank[i * 8 + u] = -1

    def slot(device, local):
        place = place_of(device ^ me, order_of(peers, spans[0][2]))
        for begin, length, z_first in spans[1:]:
            if z_first != spans[0][2]:
                here = (local >= begin) & (local < begin + length)
                place = jnp.where(here, place_of(device ^ me, order_of(peers, z_first)), place)
        return place * size + local - first

    def visit(at, found):
        fresh = rank[at] < 0

        @pl.when(fresh)
        def _():
            rank[at] = found
            tile[found] = at
            total[found] = jnp.zeros(total.shape[1:], F32)

        return found + jnp.where(fresh, 1, 0)

    def visit_far(i, found):
        p = far_list[i]
        return visit(slot(fd(p), fl(p)), found)

    def visit_near(i, found):
        p = near_list[i]
        return visit(slot(nd(p), nl(p)), found)

    found = lax.fori_loop(0, fars, visit_far, 0)
    found = lax.fori_loop(0, nears, visit_near, found)

    for load in loads:
        load.wait()

    @pl.loop(0, (fars + GROUP - 1) // GROUP)
    def _(g):
        for u in range(GROUP):
            p = far_list[g * GROUP + u]
            value = jnp.dot(basis_in[p], source[fs(p)], preferred_element_type=F32)
            coefficients[g * GROUP + u] = jnp.concatenate(pieces(value, 2), axis=0)

    @pl.loop(0, (fars + GROUP - 1) // GROUP)
    def _(g):
        parts = []
        for u in range(GROUP):
            i = g * GROUP + u
            p = far_list[i]
            basis = jnp.concatenate([basis_out[p], basis_out[p]], axis=0)
            at = jnp.where(i < fars, rank[slot(fd(p), jnp.where(i < fars, fl(p), first))], spare)
            parts.append((at, lax.dot_general(basis, coefficients[i], (((0,), (0,)), ((), ())), preferred_element_type=F32)))
        for at, part in parts:
            total[at] = total[at] + part

    rows = iota(source.shape[1:], 0)

    @pl.loop(0, (nears + GROUP - 1) // GROUP)
    def _(g):
        parts = []
        for u in range(GROUP):
            i = g * GROUP + u

            @pl.when(i < nears)
            def _():
                fetch(i).wait()

        for u in range(GROUP):
            i = g * GROUP + u
            p = near_list[i]
            chosen = jnp.where(rows < count(p), source[ns(p)].astype(F32), 0.0).astype(BF16)
            at = jnp.where(i < nears, rank[slot(nd(p), jnp.where(i < nears, nl(p), first))], spare)
            parts.append((at, jnp.dot(held[i], chosen, preferred_element_type=F32)))
        for at, part in parts:
            total[at] = total[at] + part

    for clear in clears:
        clear.wait()

    def store(i):
        place, local = tile[i] // size, tile[i] % size
        out = iter(outs)
        for begin, length, _ in spans:
            begin = begin - first
            for low, high in parts:
                to = next(out)
                here = (local >= begin) & (local < begin + length) & (place >= low) & (place < high)

                @pl.when(here)
                def _(to=to, low=low, begin=begin, length=length):
                    at = (place - low) * length + local - begin
                    pltpu.make_async_copy(staged.at[i], to.at[at], tile_sems.at[i]).start()

    @pl.loop(0, found)
    def _(i):
        staged[i] = total[i].astype(BF16)
        store(i)

    @pl.loop(0, found)
    def _(i):
        pltpu.make_async_copy(staged.at[i], outs[0].at[0], tile_sems.at[i]).wait()


def dense_sums(spans, peers, table, source, basis_in, basis_out, blocks):
    near_pairs, width, _ = blocks.shape
    far_pairs, rank, _ = basis_in.shape
    depth = source.shape[2]
    size = sum(length for _, length, _ in spans)
    most = min(peers * size, near_pairs + far_pairs)
    shapes, clears, span = [], 0, 16
    for _, length, _ in spans:
        for low, high in ranges(peers):
            tiles = (high - low) * length
            shapes.append(jax.ShapeDtypeStruct((tiles, width, depth), BF16))
            clears += -(-tiles // span)
    anywhere = pl.BlockSpec(memory_space=pl.ANY)
    outs = pl.pallas_call(
        functools.partial(sums_kernel, spans, peers, near_pairs, far_pairs),
        out_shape=tuple(shapes),
        in_specs=[smem()] + [pl.BlockSpec(memory_space=pltpu.HBM)] * 4,
        out_specs=(anywhere,) * len(shapes),
        scratch_shapes=[
            pltpu.VMEM((most + 1, width, depth), F32),
            pltpu.VMEM((near_pairs + GROUP, width, width), BF16),
            pltpu.VMEM((far_pairs + GROUP, 2 * rank, depth), BF16),
            pltpu.VMEM((span, width, depth), BF16),
            pltpu.VMEM((most, width, depth), BF16),
            pltpu.VMEM(source.shape, BF16),
            pltpu.VMEM(basis_in.shape, BF16),
            pltpu.VMEM(basis_out.shape, BF16),
            pltpu.SMEM((near_pairs + GROUP + 1,), I32),
            pltpu.SMEM((far_pairs + GROUP + 1,), I32),
            pltpu.SMEM((peers * size,), I32),
            pltpu.SMEM((most,), I32),
            pltpu.SemaphoreType.DMA((3,)),
            pltpu.SemaphoreType.DMA((near_pairs,)),
            pltpu.SemaphoreType.DMA((clears,)),
            pltpu.SemaphoreType.DMA((most,)),
        ],
        compiler_params=pltpu.CompilerParams(vmem_limit_bytes=VMEM_BYTES),
        cost_estimate=NO_COST,
        name="dense_sums",
    )(table, source, basis_in, basis_out, blocks)
    got = []
    for j, (_, length, _) in enumerate(spans):
        tile = (length, width, depth)
        leads = ((peers // 4,), (peers // 4,), (peers // 2,))
        got.append([out.reshape(lead + tile) for out, lead in zip(outs[3 * j : 3 * j + 3], leads)])
    return got


def pack_kernel(volume, stiffness, out):
    planes, cy, cz = volume.shape
    lanes = iota((cy, cz), 1)
    packed = jnp.zeros((cy, cz), F32)
    rows = iota((cy, cz), 0)

    def place(packed, column, at):
        return jnp.where(lanes == at, column, packed)

    for x in range(planes):
        here = volume[x]
        beside = jnp.where(rows == 0, 0.0, pltpu.roll(here, 1, 0))
        beside = beside + jnp.where(rows == cy - 1, 0.0, pltpu.roll(here, cy - 1, 0))
        if x > 0:
            beside = beside + volume[x - 1]
        if x < planes - 1:
            beside = beside + volume[x + 1]
        face = (6.0 + stiffness[x]) * here - beside
        column = face[:, 0:1] - here[:, 1:2]
        packed = place(packed, column, x)
    packed = place(packed, volume[0][:, 0:1], planes)
    packed = place(packed, volume[planes - 1][:, 0:1], planes + 1)
    packed = packed.T[: out.shape[1]]
    for n in range(out.shape[0]):
        out[n] = packed


def pack_face(peers, volume, stiffness):
    planes, cy, cz = volume.shape
    return pl.pallas_call(
        pack_kernel,
        out_shape=jax.ShapeDtypeStruct((peers, -(-(planes + 2) // 8) * 8, cy), F32),
        in_specs=[vmem()] * 2,
        out_specs=vmem(),
        compiler_params=pltpu.CompilerParams(vmem_limit_bytes=VMEM_BYTES),
        cost_estimate=NO_COST,
        name="pack_face",
    )(volume, stiffness)


def stencil_kernel(volume, stiffness, before, after, out):
    planes, cy, cz = volume.shape
    rows = iota((cy, cz), 0)
    lanes = iota((cy, cz), 1)
    for x in range(planes):
        here = volume[x]
        beside = (volume[x + 1] if x < planes - 1 else after[0]) + (volume[x - 1] if x > 0 else before[0])
        beside = beside + jnp.where(rows == cy - 1, 0.0, pltpu.roll(here, cy - 1, 0))
        beside = beside + jnp.where(rows == 0, 0.0, pltpu.roll(here, 1, 0))
        beside = beside + jnp.where(lanes == cz - 1, 0.0, pltpu.roll(here, cz - 1, 1))
        beside = beside + jnp.where(lanes == 0, 0.0, pltpu.roll(here, 1, 1))
        out[x] = (6.0 + stiffness[x]) * here - beside


def stencil(volume, stiffness, before, after):
    return pl.pallas_call(
        stencil_kernel,
        out_shape=jax.ShapeDtypeStruct(volume.shape, F32),
        in_specs=[vmem()] * 4,
        out_specs=vmem(),
        compiler_params=pltpu.CompilerParams(vmem_limit_bytes=VMEM_BYTES),
        cost_estimate=NO_COST,
        name="stencil",
    )(volume, stiffness, before, after)


def trace_kernel(
    ns, target, count, packs, places, far_blocks, basis_in, basis_out, far_source, far_target,
    traces, images, face, near_blocks, sem,
):
    load = pltpu.make_async_copy(far_blocks, near_blocks, sem)
    load.start()
    peers, _, cy = packs.shape
    nx = face.shape[0]
    planes = nx // peers
    clusters, width = places.shape
    rows8 = iota((planes, cy), 0)
    for n in range(peers):
        part = packs[n, 0:planes, :]
        if n > 0:
            part = part - jnp.where(rows8 == 0, packs[n - 1, planes + 1 : planes + 2, :], 0.0)
        if n < peers - 1:
            part = part - jnp.where(rows8 == planes - 1, packs[n + 1, planes : planes + 1, :], 0.0)
        face[n * planes : (n + 1) * planes, :] = part
    turned = jnp.concatenate(pieces(face[...].T, 3), axis=0)
    x_rows = iota((nx, width), 0)
    y_rows = iota((cy, width), 0)
    shift = cy.bit_length() - 1

    @pl.loop(0, clusters, unroll=4)
    def _(c):
        place = places[pl.ds(c, 1), :]
        picks = jnp.where(x_rows == (place >> shift), 1.0, 0.0).astype(BF16)
        columns = jnp.dot(turned, picks, preferred_element_type=F32)
        columns = columns[:cy] + columns[cy : 2 * cy] + columns[2 * cy :]
        found = jnp.where(y_rows == (place & (cy - 1)), columns, 0.0)
        traces[pl.ds(c, 1), :] = jnp.sum(found, axis=0, keepdims=True)

    contract = (((1,), (1,)), ((), ()))
    stacked = jnp.concatenate(pieces(traces[...], 2), axis=0)
    coefficients = lax.dot_general(stacked, basis_in[...], contract, preferred_element_type=F32)
    coefficients = coefficients[:clusters] + coefficients[clusters:]
    pairs_k = coefficients.shape[1]
    coefficients = jnp.where(iota((clusters, pairs_k), 0) == far_source[...], coefficients, 0.0)
    coefficients = jnp.sum(coefficients, axis=0, keepdims=True)
    block = 128

    @pl.loop(0, images.shape[0] // block)
    def _(b):
        base = pl.multiple_of(b * block, block)
        spread = jnp.where(iota((block, pairs_k), 0) + base == far_target[...], coefficients, 0.0)
        image = jnp.zeros((block, width), F32)
        for part in pieces(spread, 2):
            image = image + jnp.dot(part, basis_out[...], preferred_element_type=F32)
        images[pl.ds(base, block), :] = image

    lanes = iota((8, width), 1)
    rows = iota((8, width), 0)
    load.wait()
    group = math.gcd(near_blocks.shape[0], GROUP)

    @pl.loop(0, near_blocks.shape[0] // group)
    def _(g):
        parts = []
        for u in range(group):
            p = g * group + u
            at = target[p]
            trace = traces[pl.ds(ns[p], 1), :]
            placed = jnp.where((rows == (at & 7)) & (lanes < count[p]), trace, 0.0)
            both = jnp.concatenate(pieces(placed, 2), axis=0)
            image = lax.dot_general(both, near_blocks[p], contract, preferred_element_type=F32)
            parts.append((pl.multiple_of((at >> 3) * 8, 8), image[:8] + image[8:]))
        for base, image in parts:
            images[pl.ds(base, 8), :] = images[pl.ds(base, 8), :] + image


def trace_images(peers, nx, ns, target, count, packs, places, near_blocks, basis_in, basis_out, far_source, far_target):
    clusters, width = places.shape
    pairs, rank, _ = basis_in.shape
    return pl.pallas_call(
        trace_kernel,
        out_shape=(
            jax.ShapeDtypeStruct((clusters, width), F32),
            jax.ShapeDtypeStruct((peers * clusters, width), F32),
        ),
        in_specs=[smem()] * 3 + [vmem()] * 2 + [pl.BlockSpec(memory_space=pl.ANY)] + [vmem()] * 4,
        out_specs=(vmem(), vmem()),
        scratch_shapes=[
            pltpu.VMEM((nx, packs.shape[2]), F32),
            pltpu.VMEM(near_blocks.shape, BF16),
            pltpu.SemaphoreType.DMA(()),
        ],
        compiler_params=pltpu.CompilerParams(vmem_limit_bytes=VMEM_BYTES),
        cost_estimate=NO_COST,
        name="trace_images",
    )(
        ns, target, count, packs, places, near_blocks,
        basis_in.reshape(pairs * rank, width), basis_out.reshape(pairs * rank, width),
        jnp.repeat(far_source, rank)[None, :], jnp.repeat(far_target, rank)[None, :],
    )


def sum_kernel(groups, *refs):
    outs = refs[len(refs) - len(groups) :]
    for out, group in zip(outs, groups):
        total = None
        for operand, index in group:
            term = refs[operand][index].astype(F32)
            total = term if total is None else total + term
        out[...] = total.astype(out.dtype)


def tile_sums(grid, groups, operands, outputs, aliases={}):
    return pl.pallas_call(
        functools.partial(sum_kernel, groups),
        grid=(grid,),
        out_shape=tuple(shape for shape, _, _ in outputs),
        in_specs=[pl.BlockSpec(block, index) for _, block, index in operands],
        out_specs=tuple(pl.BlockSpec(block, index) for _, block, index in outputs),
        input_output_aliases=aliases,
        compiler_params=pltpu.CompilerParams(vmem_limit_bytes=VMEM_BYTES),
        cost_estimate=NO_COST,
        name="tile_sums",
    )(*[array for array, _, _ in operands])


def block_of(size, most):
    return max(d for d in range(1, max(1, min(size, most)) + 1) if size % d == 0)


def half_sum(keep, other):
    places, tile = other.shape[0], other.shape[1:]
    step = max(1, places // 2)
    zeros = (0,) * len(tile)
    block = (step,) + tile
    return tile_sums(
        places // step, [[(0, ...), (1, ...)]],
        [(keep, block, lambda i: (places // step + i,) + zeros), (other, block, lambda i: (i,) + zeros)],
        [(jax.ShapeDtypeStruct(other.shape, BF16), block, lambda i: (i,) + zeros)],
    )[0]


def later_sum(places, *terms):
    size, width, depth = terms[0].shape[1:]
    step = block_of(size, 10 // places)
    block = (places, step, width, depth)
    return tile_sums(
        size // step, [[(i, ...) for i in range(len(terms))]],
        [(term, block, lambda i: (1, i, 0, 0)) for term in terms],
        [(jax.ShapeDtypeStruct((places, size, width, depth), BF16), block, lambda i: (0, i, 0, 0))],
    )[0]


def result(first, out, *terms):
    size, width, depth = terms[0].shape[1:]
    step = block_of(size, 5)
    while first % step:
        step = block_of(size, step - 1)
    tile = (step, width, depth)
    here = (out, tile, lambda i: (first // step + i, 0, 0))
    operands = [here] + [(term, (None,) + tile, lambda i: (0, i, 0, 0)) for term in terms]
    return tile_sums(
        size // step, [[(i, ...) for i in range(len(operands))]], operands,
        [(jax.ShapeDtypeStruct(out.shape, F32),) + here[1:]], {0: 0},
    )[0]


def swap(value, bit):
    peers = lax.axis_size("clus")
    return lax.ppermute(value, "clus", [(i, i ^ bit) for i in range(peers)])


class Sent:
    def __init__(self, value):
        self.value = value


class Order:
    def __init__(self, token):
        self.token = token
        self.sent, self.later, self.late = [], [], False

    def send(self, value):
        sent = Sent(value)
        (self.later if self.late else self.sent).append(sent)
        return sent

    def wait(self):
        values = self(lambda *a: a, *[sent.value for sent in self.sent])
        for sent, value in zip(self.sent, values):
            sent.value = value
        self.sent, self.later = self.later, []

    def __call__(self, act, *args):
        args, _ = lax.optimization_barrier((args, self.token))
        out = act(*args)
        self.token = jax.tree.leaves(out)[0]
        return out


def body(
    adjoint_volume,
    stiffness,
    boundary_source,
    trace_gain,
    trace_map,
    near_blocks,
    near_source,
    near_target_dev,
    near_target_local,
    close_block_column_count,
    far_basis_in,
    far_basis_out,
    far_source,
    far_target_dev,
    far_target_local,
):
    peers = lax.axis_size("clus")
    clusters = boundary_source.shape[0]
    planes = adjoint_volume.shape[0]
    near_owner = near_target_dev.reshape(-1)
    far_owner = far_target_dev.reshape(-1)
    table = jnp.concatenate([
        near_source, near_owner, near_target_local, close_block_column_count,
        far_source, far_owner, far_target_local,
    ])
    near_target = near_owner * clusters + near_target_local
    far_target = far_owner * clusters + far_target_local
    order = Order(table)
    got = {}

    def sums():
        for call in range(1 + max(call for _, _, call in PLAN)):
            chunks = [j for j, plan in enumerate(PLAN) if plan[2] == call]
            pairs = order(
                lambda *a: dense_sums([spans[j] for j in chunks], peers, *a),
                table, boundary_source, far_basis_in, far_basis_out, near_blocks,
            )
            for j, pair in zip(chunks, pairs):
                got[j] = pair
            yield

    def chunk(j):
        same, other, keep = got[j]
        bits = order_of(peers, PLAN[j][1])[1:]
        other, same = order.send(swap(other, 1)), order.send(swap(same, 1))
        yield
        sent = [order.send(swap(order(half_sum, keep, other.value), bits[0]))]
        yield
        places = peers // 8
        for step, bit in enumerate(bits[1:]):
            terms = [keep, same.value] + [each.value for each in sent]
            sent.append(order.send(swap(order(functools.partial(later_sum, places), *terms), bit)))
            if step == 0 or places == 1:
                yield
            places //= 2
        terms = [keep, same.value] + [each.value for each in sent]
        got["out"] = order(functools.partial(result, spans[j][0]), got["out"], *terms)
        yield

    def exchange(value):
        return order.send(lax.all_to_all(value, "clus", split_axis=0, concat_axis=0, tiled=True))

    def face():
        packs = exchange(order(functools.partial(pack_face, peers), adjoint_volume, stiffness))
        yield
        traces, images = order(
            lambda packs, near: trace_images(
                peers, planes * peers, near_source, near_target, close_block_column_count,
                packs, trace_map, near, far_basis_in, far_basis_out, far_source, far_target,
            ),
            packs.value, near_blocks,
        )
        images = exchange(images.reshape((peers, clusters) + images.shape[1:]))
        yield
        got["out"] = order(
            lambda out, g, t, i: out + (t + jnp.sum(i, axis=0))[:, :, None] * g[None, None, :],
            got["out"], trace_gain, traces, images.value,
        )
        yield

    def base():
        got["out"] = order(lambda s: s.astype(F32), boundary_source)
        yield

    def volume():
        ends = peers - 1
        tail, head = order(lambda v: (v[planes - 1 :], v[:1]), adjoint_volume)
        before = order.send(lax.ppermute(tail, "clus", [(i, i + 1) for i in range(ends)]))
        after = order.send(lax.ppermute(head, "clus", [(i + 1, i) for i in range(ends)]))
        yield
        got["volume"] = order(stencil, adjoint_volume, stiffness, before.value, after.value)
        yield

    spans, first = [], 0
    for share, z_first, _ in PLAN:
        spans.append((first, share * clusters // 16, z_first))
        first += spans[-1][1]
    runs = {"s": sums(), "f": face(), "v": volume(), "b": base()}
    runs.update((str(j), chunk(j)) for j in range(len(PLAN)))
    for name in SEQUENCE:
        if name == "w":
            order.wait()
        elif name != "l":
            next(runs[name])
        order.late = name == "l"
    return got["volume"], got["out"]


def solution(mesh):
    whole = ("groups", "clus")
    one, two, three = P(whole), P(whole, None), P(whole, None, None)
    return jax.shard_map(
        body,
        mesh=mesh,
        in_specs=(three, three, three, P(), two, three, one, two, one, one, three, three, one, two, one),
        out_specs=(three, three),
        check_vma=False,
    )
```
